512 devices in a mesh: grp: 32 (over x, y), seq: 16 (over z, core).
Axes of the slice: x: 4, y: 8, z: 8, core: 2. Of those that a mesh axis runs over, the one named last changes fastest.
Arguments:
- tokens: bfloat16 [131072, 512], P(('grp', 'seq')), parts along dimension 0, may hold values from -6 to 6
- group_pos: int32 [32768], P('grp'), parts along dimension 0, may hold values from 0 to 4095, as said below
- log_decay: float32 [131072, 16], P(('grp', 'seq')), parts along dimension 0, may hold values from -1 to 0, as said below
- in_weight: bfloat16 [512, 2176], replicated, may hold values from -0.25 to 0.25
- norm_gain: float32 [1024], replicated, may hold values from 0.1 to 1.9
- out_weight: bfloat16 [1024, 512], replicated, may hold values from -0.1875 to 0.1875
- inner_gain: float32 [512], replicated, may hold values from 0.1 to 1.9
- qkv_weight: bfloat16 [16, 512, 192], P('seq'), may hold values from -1 to 1
- attn_out: bfloat16 [16, 64, 512], P('seq'), may hold values from -0.1875 to 0.1875
Outputs:
- result: bfloat16 [131072, 512], P(('grp', 'seq')), parts along dimension 0
The draws below stay inside these ranges and needn't reach their ends.
There are 32 independent parts, one for each index of `grp`. The reference program is written for one: setup_inputs(seed, part) draws one part's arguments, and reference() takes and returns one part's arrays. A program takes and returns all parts, laid end to end along the dimension named above; an argument that names none is the same for every part. Nothing has to cross between parts.
Inputs may be any that keep to these rules, and one draw needn't show every extreme that they name: `group_pos`: strictly increasing. Each device's 256 positions hold at least one group start and at most 128; some device holds exactly 128. `log_decay`: negative at every position.
All inputs are finite; a program needn't handle non-finite values.
Results may differ from the reference program's by a relative error of at most 0.0061.
Values may be sent and summed in bfloat16 or wider, within the bound.
A program may use at most 64 MiB of HBM per device.

```python
import jax
import jax.numpy as jnp
from jax import lax

D = 512
E = 1024
HEADS = 16
HDIM = 64
NSTATE = 64
IHDIM = 64
TOK_DEV = 256
IHEADS = 16
IDIM = 1024
SPAN_EXTENT = 4096
CH_DEV = 64
MOST = 128
NCH = 1024
N_SEQ = 16


def draw_group_pos(key, part):
    first, second, third = jax.random.split(jax.random.fold_in(key, 11), 3)
    heavy = jax.random.randint(first, (), 0, N_SEQ)
    devices = jnp.arange(N_SEQ, dtype=jnp.int32)
    weights = jax.random.randint(second, (N_SEQ,), 1, 9)
    weights = jnp.where(devices == heavy, 0, weights)
    total_w = jnp.sum(weights)
    cuts = CH_DEV * weights // total_w
    remain = CH_DEV - jnp.sum(cuts)
    ranked = jnp.cumsum((weights > 0).astype(jnp.int32)) - 1
    extra = ((weights > 0) & (ranked < remain)).astype(jnp.int32)
    counts = jnp.where(devices == heavy, MOST, CH_DEV - cuts - extra)
    scores = jax.random.randint(third, (N_SEQ, TOK_DEV), 0, 2 ** 20) * TOK_DEV + jnp.arange(TOK_DEV, dtype=jnp.int32)[None, :]
    order = jnp.argsort(scores, axis=1)
    ranks = jnp.argsort(order, axis=1)
    chosen = ranks < counts[:, None]
    return jnp.nonzero(chosen.reshape(-1), size=NCH)[0].astype(jnp.int32)


def draw_log_decay(key, part):
    kf, kr, kq, kp, lookup_segment, lookup_segment_alias, kblk = jax.random.split(jax.random.fold_in(key, 17), 7)
    fast_share = 0.5
    fast = jax.random.uniform(kf, (HEADS,)) < fast_share
    slow_rate = jax.random.uniform(kr, (HEADS,), jnp.float32, 0.1, 0.35) / SPAN_EXTENT
    fast_rate = jax.random.uniform(kq, (HEADS,), jnp.float32, 1.0 / 50.0, 1.0 / 30.0)
    fading_factor = jnp.where(fast, fast_rate, slow_rate)
    approximate_estimate = jax.random.uniform(kp, (SPAN_EXTENT, HEADS), jnp.float32, 0.5, 1.5)
    segment_sequence = jnp.exp(jax.random.uniform(kblk, (N_SEQ, 1, HEADS), jnp.float32, -0.69, 0.69))
    segment_sequence = jnp.broadcast_to(segment_sequence, (N_SEQ, TOK_DEV, HEADS)).reshape(SPAN_EXTENT, HEADS)
    spike_locations = jax.random.randint(lookup_segment, (2,), 0, SPAN_EXTENT)
    spike_magnitude = jax.random.uniform(lookup_segment_alias, (2,), jnp.float32, 0.22, 0.51)
    spike_indicator = jnp.sum((jnp.arange(SPAN_EXTENT)[:, None] == spike_locations[None, :]).astype(jnp.float32) * spike_magnitude[None, :], axis=1)
    return -(fading_factor[None, :] * approximate_estimate * segment_sequence) - spike_indicator[:, None]


def draw_qkv_weight(key, part):
    first = jax.random.fold_in(jax.random.fold_in(key, 23), 0)
    base = jax.random.normal(first, (IHEADS, D, 3 * IHDIM), jnp.float32) * D ** (-0.5)
    return jnp.clip(base, -1.0, 1.0).astype(jnp.bfloat16)


def block_scale(stream_key, extent, shards, smallest, top_value):
    factor_of = 1.0
    for axis_at, parts in shards:
        draws = jax.random.uniform(jax.random.fold_in(jax.random.fold_in(stream_key, 6), axis_at), (parts,), jnp.float32, smallest / len(shards), top_value / len(shards))
        factor_of = factor_of * jnp.repeat(jnp.exp(draws), extent[axis_at] // parts).reshape((-1,) + (1,) * (len(extent) - 1 - axis_at))
    return factor_of


def normal_values(stream_key, shape, scale, reach, cuts=(), kind=jnp.bfloat16):
    loudness = block_scale(stream_key, shape, cuts, -0.22, 0.18) if cuts else 1.0
    drawn = jax.random.normal(stream_key, shape, jnp.float32) * scale * loudness
    return jnp.minimum(jnp.maximum(drawn, -reach), reach).astype(kind)


def setup_inputs(seed: int = 0, part: int = 0) -> dict:
    seeds = jax.random.split(jax.random.key(seed), 10)
    part_keys = jax.random.split(jax.random.fold_in(seeds[9], part), 10)
    return {
        "tokens": normal_values(part_keys[0], (SPAN_EXTENT, D), 1.0, 6.0, ((0, 16),)),
        "group_pos": draw_group_pos(jax.random.fold_in(jax.random.fold_in(seeds[9], part), 71), part),
        "log_decay": draw_log_decay(jax.random.fold_in(jax.random.fold_in(seeds[9], part), 71), part),
        "in_weight": normal_values(seeds[3], (D, 2 * E + 2 * NSTATE), D ** -0.5, 0.25),
        "norm_gain": jnp.clip(1.0 + 0.18 * jax.random.normal(seeds[4], (E,), jnp.float32), 0.1, 1.9),
        "out_weight": normal_values(seeds[5], (E, D), E ** -0.5, 0.1875),
        "inner_gain": jnp.clip(1.0 + 0.18 * jax.random.normal(seeds[6], (D,), jnp.float32), 0.1, 1.9),
        "qkv_weight": draw_qkv_weight(jax.random.fold_in(seeds[9], 71), part),
        "attn_out": normal_values(seeds[8], (IHEADS, IHDIM, D), IDIM ** -0.5, 0.1875, ((0, 16),)),
    }


def rms_norm(values, gain):
    return values * lax.rsqrt(lax.optimization_barrier(jnp.mean(values * values, axis=-1, keepdims=True)) + 1e-05) * gain

def reference(tokens, group_pos, log_decay, in_weight, norm_gain, out_weight, inner_gain, qkv_weight, attn_out):
    proj = jnp.dot(tokens, in_weight, preferred_element_type=jnp.float32).astype(jnp.bfloat16)
    xs = proj[:, :E].astype(jnp.float32).reshape(SPAN_EXTENT, HEADS, HDIM)
    gate = proj[:, E:2 * E].astype(jnp.float32)
    bmat = proj[:, 2 * E:2 * E + NSTATE].astype(jnp.float32)
    cmat = proj[:, 2 * E + NSTATE:].astype(jnp.float32)

    def advance(state, inputs):
        decay, xrow, brow, crow = inputs
        state = jnp.exp(decay)[:, None, None] * state + xrow[:, :, None] * brow[None, None, :]
        out = jnp.einsum('hpn,n->hp', state, crow, precision=lax.Precision.HIGHEST)
        return (state, out)
    start = jnp.zeros((HEADS, HDIM, NSTATE), jnp.float32)
    _, ys = lax.scan(advance, start, (log_decay, xs, bmat, cmat))
    gated = ys.reshape(SPAN_EXTENT, E) * jax.nn.silu(gate)
    normed = rms_norm(gated, norm_gain).astype(jnp.bfloat16)
    hidden = (tokens.astype(jnp.float32) + jnp.dot(normed, out_weight, preferred_element_type=jnp.float32)).astype(jnp.bfloat16)
    rows = hidden[group_pos].astype(jnp.float32)
    rows_n = rms_norm(rows, inner_gain).astype(jnp.bfloat16)
    causal = jnp.arange(NCH)[:, None] >= jnp.arange(NCH)[None, :]

    def one_head(total, weights):
        w_qkv, w_out = weights
        qkv = jnp.dot(rows_n, w_qkv, preferred_element_type=jnp.float32).astype(jnp.bfloat16)
        query = qkv[:, :IHDIM]
        keys = qkv[:, IHDIM:2 * IHDIM]
        values = qkv[:, 2 * IHDIM:]
        scores = jnp.dot(query, keys.T, preferred_element_type=jnp.float32) * IHDIM ** (-0.5)
        scores = jnp.where(causal, scores, -jnp.inf)
        top = lax.optimization_barrier(jnp.max(scores, axis=1, keepdims=True))
        expo = jnp.exp(scores - top)
        probs = (expo / lax.optimization_barrier(jnp.sum(expo, axis=1, keepdims=True))).astype(jnp.bfloat16)
        heads_out = jnp.dot(probs, values, preferred_element_type=jnp.float32).astype(jnp.bfloat16)
        return (total + jnp.dot(heads_out, w_out, preferred_element_type=jnp.float32), None)
    back, _ = lax.scan(one_head, jnp.zeros((NCH, D), jnp.float32), (qkv_weight, attn_out))
    return hidden.astype(jnp.float32).at[group_pos].add(back).astype(jnp.bfloat16)
```

```python
import jax
import jax.numpy as jnp
from jax import lax
from jax.experimental import pallas as pl
from jax.experimental.pallas import tpu as pltpu
from jax.sharding import PartitionSpec as P

MESH = pl.DeviceIdType.MESH
F32 = jnp.float32
BF16 = jnp.bfloat16

N = 16
RING = 8
TOK = 256
SUB = 128
D = 512
E = 1024
HEADS = 16
HDIM = 64
NST = 64
NG = 1024
MOST = 128
HALF = MOST // 2
QB = 256
BAND = QB + NG


def dot(a, b):
    return jnp.dot(a, b, preferred_element_type=F32)


def dot_nt(a, b):
    return lax.dot_general(a, b, (((1,), (1,)), ((), ())), preferred_element_type=F32)


def dot_tn(a, b):
    return lax.dot_general(a, b, (((0,), (0,)), ((), ())), preferred_element_type=F32)


def iota(shape, dim):
    return lax.broadcasted_iota(jnp.int32, shape, dim)


def two_terms(x):
    high = x.astype(BF16)
    return high, (x - high.astype(F32)).astype(BF16)


def spread(x, table):
    high, low = two_terms(x)
    return dot(high, table) + dot(low, table)


def layer(
    tokens,
    gpos,
    decay,
    w_in,
    gain,
    w_out,
    inner,
    w_qkv,
    w_back,
    out,
    total,
    pieces,
    arrived,
    states,
    state_in,
    proj,
    xs,
    inner_y,
    factor,
    hidden,
    place,
    rows,
    backs,
    qkv,
    packed,
    pick,
    outs,
    sent,
    heads,
    s_tot,
    r_tot,
    s_p,
    r_p,
    s_s,
    r_s,
    s_g,
    r_g,
    s_gs,
    r_gs,
    s_w,
    r_w,
    s_ws,
    r_ws,
    s_h,
    r_h,
):
    me = lax.axis_index("seq")
    chip = me // 2
    core = lax.rem(me, 2)
    sibling = chip * 2 + (1 - core)

    def on_ring(step):
        return lax.rem(chip + step + RING, RING) * 2 + core

    def remote(src, dst, s_sem, r_sem, to):
        return pltpu.make_async_remote_copy(
            src_ref=src,
            dst_ref=dst,
            send_sem=s_sem,
            recv_sem=r_sem,
            device_id={"seq": to},
            device_id_type=MESH,
        )

    def others(body):
        lax.fori_loop(1, N, lambda k, c: (body(lax.rem(me + k, N)), c)[1], 0)

    barrier = pltpu.get_barrier_semaphore()
    others(lambda d: pl.semaphore_signal(barrier, inc=1, device_id={"seq": d}, device_id_type=MESH))

    ld = decay[...]
    tri = (iota((TOK, TOK), 0) >= iota((TOK, TOK), 1)).astype(BF16)
    first, rest = two_terms(ld)
    second, third = two_terms(ld - first.astype(F32))
    cum = dot(tri, first) + dot(tri, second) + dot(tri, third)
    end = cum[TOK - 1 : TOK]
    total[me] = jnp.broadcast_to(jnp.pad(end, ((0, 0), (0, 128 - HEADS))), (8, 128))
    backs[me] = w_back[0]

    pl.semaphore_wait(barrier, N - 1)
    tot_copy = lambda d, src: remote(total.at[src], total.at[src], s_tot.at[d], r_tot.at[src], d)
    others(lambda d: tot_copy(d, me).start())

    def ring_send(buf, half, s_sem, r_sem, block, part, way, slot):
        ref = buf.at[block, pl.ds(part * half, half), :]
        return remote(ref, ref, s_sem.at[slot], r_sem.at[2 * block + part], on_ring(way))

    def ring_slot(step, part, way):
        return (step * 2 + part) * 2 + (way + 1) // 2

    def ring_step(buf, half, s_sem, r_sem, s_sib, r_sib, step):
        for part in range(2):
            for way in (1, -1):
                last = step == RING // 2
                if last and (part == 0) != (way == 1):
                    continue
                block = on_ring(-way * step)
                if step > 0:
                    ring_send(buf, half, s_sem, r_sem, block, part, way, 0).wait_recv()
                if step < RING // 2 - 1 or (step == RING // 2 - 1 and (part == 0) == (way == 1)):
                    ring_send(buf, half, s_sem, r_sem, block, part, way, ring_slot(step, part, way)).start()
        for way in (1, -1) if 0 < step < RING // 2 else (1,):
            block = on_ring(-way * step)
            remote(buf.at[block], buf.at[block], s_sib.at[block // 2], r_sib.at[block // 2], sibling).start()

    def ring_sibling_wait(buf, s_sib, r_sib, step):
        for way in (1, -1) if 0 < step < RING // 2 else (1,):
            block = on_ring(-way * step)
            other = (block // 2) * 2 + (1 - core)
            remote(buf.at[other], buf.at[other], s_sib.at[block // 2], r_sib.at[block // 2], sibling).wait_recv()

    def ring_done(buf, half, s_sem, r_sem, s_sib, r_sib):
        for step in range(RING // 2):
            for part in range(2):
                for way in (1, -1):
                    if step < RING // 2 - 1 or (part == 0) == (way == 1):
                        block = on_ring(-way * step)
                        ring_send(buf, half, s_sem, r_sem, block, part, way, ring_slot(step, part, way)).wait_send()
        for b in range(RING):
            block = b * 2 + core
            remote(buf.at[block], buf.at[block], s_sib.at[b], r_sib.at[b], sibling).wait_send()

    back_ring = (backs, HDIM // 2, s_w, r_w, s_ws, r_ws)
    row_ring = (rows, HALF, s_g, r_g, s_gs, r_gs)
    ring_step(*back_ring, 0)

    toks = tokens[...]
    for c in range(0, 2 * E + 2 * NST, 256):
        w = min(256, 2 * E + 2 * NST - c)
        proj[:, c : c + w] = dot(toks, w_in[:, c : c + w]).astype(BF16)

    mids = [cum[SUB // 2 - 1 : SUB // 2], cum[SUB + SUB // 2 - 1 : SUB + SUB // 2]]
    rel = jnp.concatenate([cum[:SUB] - mids[0], cum[SUB:] - mids[1]], axis=0)
    table = (iota((HEADS, E), 1) // HDIM == iota((HEADS, E), 0)).astype(BF16)
    f_in = spread(jnp.exp(rel), table)
    f_out = spread(jnp.exp(-rel), table)
    few = jnp.concatenate(
        [mids[0], mids[1], end - mids[0], end - mids[1], mids[1] - mids[0], end, end, end], axis=0
    )
    few = spread(jnp.exp(few), table)
    xs[...] = (proj[:, :E].astype(F32) * f_out).astype(BF16)
    bc = proj[:, 2 * E :]
    bmat, cmat = bc[:, :NST], bc[:, NST:]
    low = iota((SUB, SUB), 0) >= iota((SUB, SUB), 1)
    u = [dot_tn(bmat[k * SUB : (k + 1) * SUB], xs[k * SUB : (k + 1) * SUB]) for k in range(2)]
    local = (u[0] * few[2:3] + u[1] * few[3:4]).astype(BF16)
    for d in range(N):
        r, c = 16 * (d // 4), 256 * (d % 4)
        pieces[d] = local[r : r + 16, c : c + 256]

    p_copy = lambda d, src: remote(pieces.at[d], arrived.at[src], s_p.at[d], r_p.at[src], d)
    others(lambda d: p_copy(d, me).start())
    arrived[me] = pieces[me]

    u0 = (u[0] * few[4:5]).astype(BF16)
    for k in range(2):
        b_k, c_k = bmat[k * SUB : (k + 1) * SUB], cmat[k * SUB : (k + 1) * SUB]
        g = jnp.where(low, dot_nt(c_k, b_k), 0.0).astype(BF16)
        y = dot(g, xs[k * SUB : (k + 1) * SUB])
        if k == 1:
            y = y + dot(c_k, u0)
        inner_y[k * SUB : (k + 1) * SUB] = y
    gate = proj[:, E : 2 * E].astype(F32)
    factor[...] = f_in * (gate / (1.0 + jnp.exp(-gate)))

    others(lambda d: tot_copy(d, d).wait_recv())
    lanes = iota((128, 256), 1) // HDIM + 4 * lax.rem(me, 4)
    mine = (lanes == iota((128, 256), 0)).astype(BF16)
    sums = jnp.concatenate([total[d][0:1] for d in range(N)], axis=0)
    fades = spread(jnp.exp(sums), mine)

    others(lambda d: p_copy(d, d).wait_recv())
    run = jnp.zeros((16, 256), F32)
    for d in range(N):
        states[d] = run.astype(BF16)
        run = run * fades[d : d + 1] + arrived[d].astype(F32)
    s_copy = lambda d, src: remote(states.at[d], state_in.at[src], s_s.at[d], r_s.at[src], d)
    others(lambda d: s_copy(d, me).start())
    state_in[me] = states[me]

    ring_step(*back_ring, 1)

    gp = gpos[...]
    base = me * TOK
    before = [jnp.sum((gp < d * TOK).astype(jnp.int32)) for d in range(N)] + [jnp.int32(NG)]
    here = jnp.sum((gp < base).astype(jnp.int32))
    at = base + iota((TOK, 128), 0)
    less = jnp.zeros((TOK, 128), F32)
    same = jnp.zeros((TOK, 128), F32)
    for r in range(8):
        row = gp[r : r + 1]
        less = less + (row < at).astype(F32)
        same = same + (row == at).astype(F32)
    ones = jnp.ones((8, 128), BF16)
    rank = dot_nt(ones, less.astype(BF16))[0:1] - here.astype(F32)
    start = dot_nt(ones, same.astype(BF16))[0:1]
    place[...] = ((rank == iota((MOST, TOK), 0).astype(F32)) & (start > 0.5)).astype(BF16)

    others(lambda d: s_copy(d, d).wait_recv())
    ring_step(*back_ring, 2)

    squares = jnp.zeros((TOK, 1), F32)
    for q in range(4):
        cols = slice(256 * q, 256 * q + 256)
        s = jnp.concatenate([state_in[4 * k + q] for k in range(4)], axis=0).astype(F32)
        s = [(s * few[k : k + 1, cols]).astype(BF16) for k in range(2)]
        carried = jnp.concatenate([dot(cmat[k * SUB : (k + 1) * SUB], s[k]) for k in range(2)], axis=0)
        gated = (inner_y[:, cols] + carried) * factor[:, cols]
        inner_y[:, cols] = gated
        squares = squares + jnp.sum(gated * gated, axis=1, keepdims=True)
    scale = lax.rsqrt(squares * (1.0 / E) + 1e-5)
    normed = (inner_y[...] * scale * gain[...]).astype(BF16)
    hid = (toks.astype(F32) + dot(normed, w_out[...])).astype(BF16)
    hidden[...] = hid
    own = dot(place[...], hid)
    own = own * lax.rsqrt(jnp.mean(own * own, axis=1, keepdims=True) + 1e-5) * inner[...]
    rows[me] = own.astype(BF16)

    ring_step(*row_ring, 0)

    lane = iota((1, MOST), 1)
    slots = [jnp.where(lane + before[d] < before[d + 1], lane + before[d], -1) for d in range(N)]
    for p in range(NG // QB):
        for t in range(BAND // MOST):
            d = p * QB // MOST + t
            want = iota((QB, MOST), 0) + p * QB
            pick[p, :, t * MOST : (t + 1) * MOST] = (want == slots[d]).astype(BF16)
    outs[...] = jnp.zeros_like(outs)

    def project(block):
        qkv[pl.ds(pl.multiple_of(block * MOST, MOST), MOST), :] = dot(rows[block], w_qkv[0]).astype(BF16)

    project(me)
    for step in range(1, RING // 2 + 1):
        ring_step(*row_ring, step)
        if step == 1:
            ring_step(*back_ring, 3)
        if step == 2:
            ring_step(*back_ring, 4)
        ring_sibling_wait(rows, s_gs, r_gs, step - 1)
        for way in (1, -1) if 0 < step - 1 < RING // 2 else (1,):
            project((on_ring(-way * (step - 1)) // 2) * 2 + 1 - core)
        for way in (1, -1) if step < RING // 2 else (1,):
            project(on_ring(-way * step))
    ring_sibling_wait(rows, s_gs, r_gs, RING // 2)
    project((on_ring(RING // 2) // 2) * 2 + 1 - core)

    for p in range(NG // QB):
        packed[p * QB : (p + 1) * QB] = dot(pick[p], qkv[p * QB : p * QB + BAND]).astype(BF16)

    h_copy = lambda d, src: remote(sent.at[d], heads.at[src], s_h.at[d], r_h.at[src], d)

    def ship(d):
        block = outs[pl.ds(before[d], MOST), :]
        sent[d] = jnp.concatenate([block[:HALF], block[HALF:]], axis=1).astype(BF16)

        @pl.when(me != d)
        def _():
            h_copy(d, me).start()

    corner = iota((QB, QB), 0) >= iota((QB, QB), 1)
    shipped = 0
    for p in range(NG // QB):
        upto = (p + 1) * QB
        query = packed[p * QB : upto, :HDIM] * jnp.asarray(HDIM**-0.5, BF16)
        scores = dot_nt(query, packed[:upto, HDIM : 2 * HDIM])
        edge = jnp.where(corner, scores[:, p * QB :], -jnp.inf)
        scores = edge if p == 0 else jnp.concatenate([scores[:, : p * QB], edge], axis=1)
        expo = jnp.exp(scores - jnp.max(scores, axis=1, keepdims=True))
        weight = 1.0 / jnp.sum(expo, axis=1, keepdims=True)
        outs[p * QB : upto] = dot(expo.astype(BF16), packed[:upto, 2 * HDIM :]) * weight
        until = N if upto == NG else upto // MOST
        for d in range(shipped, until):
            ship(d)
        shipped = until
    heads[me] = sent[me]

    for step in range(RING // 2 + 1):
        ring_sibling_wait(backs, s_ws, r_ws, step)

    others(lambda d: h_copy(d, d).wait_recv())
    left = iota((HALF, 128), 1) < HDIM
    tops, bottoms = [], []
    for h in range(0, N, 2):
        a, b = heads[h].astype(F32), heads[h + 1].astype(F32)
        tops.append(jnp.where(left, a, pltpu.roll(b, HDIM, 1)).astype(BF16))
        bottoms.append(jnp.where(left, pltpu.roll(a, HDIM, 1), b).astype(BF16))
    joined = jnp.concatenate([jnp.concatenate(tops, axis=1), jnp.concatenate(bottoms, axis=1)], axis=0)
    back = dot(joined, backs[...].reshape(N * HDIM, D))
    high, lower = two_terms(back)
    put = place[...]
    out[...] = (hidden[...].astype(F32) + dot_tn(put, high) + dot_tn(put, lower)).astype(BF16)

    others(lambda d: tot_copy(d, me).wait_send())
    others(lambda d: p_copy(d, me).wait_send())
    others(lambda d: s_copy(d, me).wait_send())
    others(lambda d: h_copy(d, me).wait_send())
    ring_done(*back_ring)
    ring_done(*row_ring)


def shards(tokens, group_pos, log_decay, in_weight, norm_gain, out_weight, inner_gain, qkv_weight, attn_out):
    vmem = pl.BlockSpec(memory_space=pltpu.VMEM)
    dma = pltpu.SemaphoreType.DMA
    return pl.pallas_call(
        layer,
        out_shape=jax.ShapeDtypeStruct((TOK, D), BF16),
        in_specs=[vmem] * 9,
        out_specs=vmem,
        scratch_shapes=[
            pltpu.VMEM((N, 8, 128), F32),
            pltpu.VMEM((N, 16, 256), BF16),
            pltpu.VMEM((N, 16, 256), BF16),
            pltpu.VMEM((N, 16, 256), BF16),
            pltpu.VMEM((N, 16, 256), BF16),
            pltpu.VMEM((TOK, 2 * E + 2 * NST), BF16),
            pltpu.VMEM((TOK, E), BF16),
            pltpu.VMEM((TOK, E), F32),
            pltpu.VMEM((TOK, E), F32),
            pltpu.VMEM((TOK, D), BF16),
            pltpu.VMEM((MOST, TOK), BF16),
            pltpu.VMEM((N, MOST, D), BF16),
            pltpu.VMEM((N, HDIM, D), BF16),
            pltpu.VMEM((N * MOST, 3 * HDIM), BF16),
            pltpu.VMEM((NG, 3 * HDIM), BF16),
            pltpu.VMEM((NG // QB, QB, BAND), BF16),
            pltpu.VMEM((NG + MOST, HDIM), F32),
            pltpu.VMEM((N, HALF, 128), BF16),
            pltpu.VMEM((N, HALF, 128), BF16),
        ]
        + [dma((N,))] * 6
        + [dma((16,)), dma((2 * N,)), dma((RING,)), dma((RING,))] * 2
        + [dma((N,))] * 2,
        compiler_params=pltpu.CompilerParams(
            collective_id=0, has_side_effects=True, vmem_limit_bytes=48 * 2**20
        ),
    )(
        tokens,
        group_pos.reshape(8, NG // 8),
        log_decay,
        in_weight,
        norm_gain.reshape(1, E),
        out_weight,
        inner_gain.reshape(1, D),
        qkv_weight,
        attn_out,
    )


def solution(mesh):
    return jax.shard_map(
        shards,
        mesh=mesh,
        in_specs=(
            P(("grp", "seq"), None),
            P("grp"),
            P(("grp", "seq"), None),
            P(),
            P(),
            P(),
            P(),
            P("seq", None, None),
            P("seq", None, None),
        ),
        out_specs=P(("grp", "seq"), None),
        check_vma=False,
    )
```

```python
import functools

import jax
import jax.numpy as jnp
from jax import lax
from jax.experimental import pallas as pl
from jax.experimental.pallas import tpu as pltpu
from jax.sharding import PartitionSpec as P

MESH = pl.DeviceIdType.MESH
F32 = jnp.float32
BF16 = jnp.bfloat16

N = 16
RING = 8
TOK = 256
SUB = 128
D = 512
E = 1024
HEADS = 16
HDIM = 64
NST = 64
NG = 1024
MOST = 128
HALF = MOST // 2
W_IN = 2 * E + 2 * NST
PARTS = 4
QB = 256
BAND = QB + NG


FAR_FIRST = sorted(range(1, N), key=lambda k: -min(k, N - k))


def dot(a, b):
    return jnp.dot(a, b, preferred_element_type=F32)


def dot_nt(a, b):
    return lax.dot_general(a, b, (((1,), (1,)), ((), ())), preferred_element_type=F32)


def dot_tn(a, b):
    return lax.dot_general(a, b, (((0,), (0,)), ((), ())), preferred_element_type=F32)


def iota(shape, dim):
    return lax.broadcasted_iota(jnp.int32, shape, dim)


def two_terms(x):
    high = x.astype(BF16)
    return high, (x - high.astype(F32)).astype(BF16)


def spread(x, table):
    high, low = two_terms(x)
    return dot(high, table) + dot(low, table)


def layer(
    tokens_h,
    gpos_h,
    decay_h,
    w_in_h,
    gain_h,
    w_out_h,
    inner_h,
    w_qkv_h,
    w_back_h,
    out,
    tokens,
    gpos,
    decay,
    w_in,
    gain,
    w_out,
    inner,
    w_qkv,
    total,
    pieces,
    arrived,
    states,
    state_in,
    proj,
    xs,
    inner_y,
    factor,
    hidden,
    place,
    rows,
    backs,
    qkv,
    packed,
    pick,
    outs,
    firsts,
    sent,
    heads,
    loaded,
    s_tot,
    r_tot,
    s_p,
    r_p,
    s_s,
    r_s,
    s_g,
    r_g,
    s_gs,
    r_gs,
    s_w,
    r_w,
    s_ws,
    r_ws,
    s_h,
    r_h,
):
    me = lax.axis_index("seq")
    chip = me // 2
    core = lax.rem(me, 2)
    sibling = chip * 2 + (1 - core)

    def on_ring(step):
        return lax.rem(chip + step + RING, RING) * 2 + core

    def remote(src, dst, s_sem, r_sem, to):
        return pltpu.make_async_remote_copy(
            src_ref=src,
            dst_ref=dst,
            send_sem=s_sem,
            recv_sem=r_sem,
            device_id={"seq": to},
            device_id_type=MESH,
        )

    def others(body):
        for k in FAR_FIRST:
            body(lax.rem(me + k, N))

    wide = [pl.ds(0, E), pl.ds(2 * E, 2 * NST), pl.ds(E, E)]
    load = {
        name: pltpu.make_async_copy(src, dst, loaded.at[k])
        for k, (name, src, dst) in enumerate(
            (
                ("decay", decay_h, decay),
                ("tokens", tokens_h, tokens),
                *((c, w_in_h.at[:, cols], w_in.at[:, cols]) for c, cols in enumerate(wide)),
                ("back", w_back_h.at[0], backs.at[me]),
                ("gpos", gpos_h, gpos),
                ("gain", gain_h, gain),
                ("out", w_out_h, w_out),
                ("inner", inner_h, inner),
                ("qkv", w_qkv_h.at[0], w_qkv),
            )
        )
    }
    late = (2, "gpos", "gain", "out", "inner", "qkv")
    for name, copy in load.items():
        if name not in late:
            copy.start()
    barrier = pltpu.get_barrier_semaphore()
    others(lambda d: pl.semaphore_signal(barrier, inc=1, device_id={"seq": d}, device_id_type=MESH))

    load["decay"].wait()
    ld = decay[...]
    tri = (iota((TOK, TOK), 0) >= iota((TOK, TOK), 1)).astype(BF16)
    first, rest = two_terms(ld)
    second, third = two_terms(ld - first.astype(F32))
    cum = dot_nt(tri, first) + dot_nt(tri, second) + dot_nt(tri, third)
    end = cum[TOK - 1 : TOK]
    total[me] = jnp.pad(end, ((0, 0), (0, 128 - HEADS)))

    pl.semaphore_wait(barrier, N - 1)
    tot_copy = lambda d, src: remote(total.at[src], total.at[src], s_tot.at[d], r_tot.at[src], d)
    others(lambda d: tot_copy(d, me).start())

    def ring_copy(ring, block, part, way, hops, slot):
        buf, parts, s_sem, r_sem, _, _ = ring
        size = buf.shape[1] // parts
        ref = buf.at[block, pl.ds(part * size, size), :]
        return remote(ref, ref, s_sem.at[slot], r_sem.at[parts * block + part], on_ring(hops * way))

    def ring_near(parts, part, way):
        return (part < parts // 2) == (way == 1)

    def ring_sends(ring, step):
        parts = ring[1]
        for part in range(parts):
            for way in (1, -1):
                slot = (step * parts + part) * 2 + (way + 1) // 2
                yield part, way, ring_copy(ring, on_ring(-way * step), part, way, 1, slot)
        for part in range(parts) if step == 2 else ():
            for way in (1, -1):
                if ring_near(parts, part, way):
                    slot = (3 * parts + part) * 2 + (way + 1) // 2
                    yield None, way, ring_copy(ring, on_ring(-way * step), part, way, 2, slot)

    def ring_wait(ring, step, part, way):
        ring_copy(ring, on_ring(-way * step), part, way, 1, 0).wait_recv()

    def ring_hand(ring, block):
        buf, _, _, _, s_sib, r_sib = ring
        return remote(buf.at[block], buf.at[block], s_sib.at[block // 2], r_sib.at[block // 2], sibling)

    def ring_ways(step):
        return (1, -1) if 0 < step < RING // 2 else (1,)

    def ring_step(ring, step):
        parts = ring[1]
        if step <= 2:
            for part, way, copy in ring_sends(ring, step):
                if step > 0 and part is not None:
                    ring_wait(ring, step, part, way)
                copy.start()
        else:
            for part in range(parts):
                for way in (1, -1):
                    if step == 3 or ring_near(parts, part, way):
                        ring_wait(ring, step, part, way)
        for way in ring_ways(step):
            ring_hand(ring, on_ring(-way * step)).start()

    def ring_sibling_wait(ring, step):
        for way in ring_ways(step):
            ring_hand(ring, (on_ring(-way * step) // 2) * 2 + 1 - core).wait_recv()

    def ring_done(ring):
        for step in range(3):
            for _, _, copy in ring_sends(ring, step):
                copy.wait_send()
        for b in range(RING):
            ring_hand(ring, b * 2 + core).wait_send()

    back_ring = (backs, 2, s_w, r_w, s_ws, r_ws)
    row_ring = (rows, PARTS, s_g, r_g, s_gs, r_gs)
    load["back"].wait()
    ring_step(back_ring, 0)

    load["tokens"].wait()
    toks = tokens[...]

    def project_in(c):
        load[c].wait()
        proj[:, wide[c]] = dot(toks, w_in[:, wide[c]]).astype(BF16)

    project_in(0)
    project_in(1)
    for name in late:
        load[name].start()

    mids = [cum[SUB // 2 - 1 : SUB // 2], cum[SUB + SUB // 2 - 1 : SUB + SUB // 2]]
    rel = jnp.concatenate([cum[:SUB] - mids[0], cum[SUB:] - mids[1]], axis=0)
    table = (iota((HEADS, E), 1) // HDIM == iota((HEADS, E), 0)).astype(BF16)
    f_in = spread(jnp.exp(rel), table)
    f_out = spread(jnp.exp(-rel), table)
    few = jnp.concatenate(
        [mids[0], mids[1], end - mids[0], end - mids[1], mids[1] - mids[0], end, end, end], axis=0
    )
    few = spread(jnp.exp(few), table)
    xs[...] = (proj[:, :E].astype(F32) * f_out).astype(BF16)
    bc = proj[:, 2 * E :]
    bmat, cmat = bc[:, :NST], bc[:, NST:]
    low = iota((SUB, SUB), 0) >= iota((SUB, SUB), 1)
    u = [dot_tn(bmat[k * SUB : (k + 1) * SUB], xs[k * SUB : (k + 1) * SUB]) for k in range(2)]
    local = (u[0] * few[2:3] + u[1] * few[3:4]).astype(BF16)
    for d in range(N):
        r, c = 16 * (d // 4), 256 * (d % 4)
        pieces[d] = local[r : r + 16, c : c + 256]

    p_copy = lambda d, src: remote(pieces.at[d], arrived.at[src], s_p.at[d], r_p.at[src], d)
    others(lambda d: p_copy(d, me).start())
    arrived[me] = pieces[me]

    load["gpos"].wait()
    gp = gpos[...]
    base = me * TOK
    before = [jnp.sum((gp < d * TOK).astype(jnp.int32)) for d in range(N)] + [jnp.int32(NG)]
    for d in range(N):
        firsts[d] = before[d]
    here = firsts[me]
    at = base + iota((TOK, 128), 0)
    less = jnp.zeros((TOK, 128), F32)
    same = jnp.zeros((TOK, 128), F32)
    for r in range(8):
        row = gp[r : r + 1]
        less = less + (row < at).astype(F32)
        same = same + (row == at).astype(F32)
    ones = jnp.ones((8, 128), BF16)
    rank = dot_nt(ones, less.astype(BF16))[0:1] - here.astype(F32)
    start = dot_nt(ones, same.astype(BF16))[0:1]
    place[...] = ((rank == iota((MOST, TOK), 0).astype(F32)) & (start > 0.5)).astype(BF16)

    u0 = (u[0] * few[4:5]).astype(BF16)
    for k in range(2):
        b_k, c_k = bmat[k * SUB : (k + 1) * SUB], cmat[k * SUB : (k + 1) * SUB]
        g = jnp.where(low, dot_nt(c_k, b_k), 0.0).astype(BF16)
        y = dot(g, xs[k * SUB : (k + 1) * SUB])
        if k == 1:
            y = y + dot(c_k, u0)
        inner_y[k * SUB : (k + 1) * SUB] = y
    project_in(2)
    gate = proj[:, E : 2 * E].astype(F32)
    factor[...] = f_in * (gate / (1.0 + jnp.exp(-gate)))

    others(lambda d: tot_copy(d, d).wait_recv())
    lanes = iota((128, 256), 1) // HDIM + 4 * lax.rem(me, 4)
    mine = (lanes == iota((128, 256), 0)).astype(BF16)
    sums = jnp.concatenate([total[d] for d in range(N)], axis=0)
    fades = spread(jnp.exp(sums), mine)

    others(lambda d: p_copy(d, d).wait_recv())
    run = jnp.zeros((16, 256), F32)
    for d in range(N):
        states[d] = run.astype(BF16)
        run = run * fades[d : d + 1] + arrived[d].astype(F32)
    s_copy = lambda d, src: remote(states.at[d], state_in.at[src], s_s.at[d], r_s.at[src], d)
    others(lambda d: s_copy(d, me).start())
    state_in[me] = states[me]

    others(lambda d: s_copy(d, d).wait_recv())
    ring_step(back_ring, 1)

    squares = jnp.zeros((TOK, 1), F32)
    for q in range(4):
        cols = slice(256 * q, 256 * q + 256)
        s = jnp.concatenate([state_in[4 * k + q] for k in range(4)], axis=0).astype(F32)
        s = [(s * few[k : k + 1, cols]).astype(BF16) for k in range(2)]
        carried = jnp.concatenate([dot(cmat[k * SUB : (k + 1) * SUB], s[k]) for k in range(2)], axis=0)
        gated = (inner_y[:, cols] + carried) * factor[:, cols]
        inner_y[:, cols] = gated
        squares = squares + jnp.sum(gated * gated, axis=1, keepdims=True)
    for name in ("gain", "out", "inner", "qkv"):
        load[name].wait()
    scale = lax.rsqrt(squares * (1.0 / E) + 1e-5)
    normed = (inner_y[...] * scale * gain[...]).astype(BF16)
    hid = (toks.astype(F32) + dot(normed, w_out[...])).astype(BF16)
    hidden[...] = hid
    own = dot(place[...], hid)
    own = own * lax.rsqrt(jnp.mean(own * own, axis=1, keepdims=True) + 1e-5) * inner[...]
    rows[me] = own.astype(BF16)

    ring_step(row_ring, 0)

    lane = iota((1, MOST), 1)
    slots = [jnp.where(lane + before[d] < before[d + 1], lane + before[d], -1) for d in range(N)]
    for p in range(NG // QB):
        for t in range(BAND // MOST):
            d = p * QB // MOST + t
            want = iota((QB, MOST), 0) + p * QB
            pick[p, :, t * MOST : (t + 1) * MOST] = (want == slots[d]).astype(BF16)
    outs[...] = jnp.zeros_like(outs)

    def project(block):
        qkv[pl.ds(pl.multiple_of(block * MOST, MOST), MOST), :] = dot_nt(rows[block], w_qkv[...]).astype(BF16)

    project(me)
    for step in range(1, RING // 2 + 1):
        ring_step(row_ring, step)
        ring_sibling_wait(row_ring, step - 1)
        for way in ring_ways(step - 1):
            project((on_ring(-way * (step - 1)) // 2) * 2 + 1 - core)
        for way in ring_ways(step):
            project(on_ring(-way * step))
    ring_sibling_wait(row_ring, RING // 2)
    project((on_ring(RING // 2) // 2) * 2 + 1 - core)
    ring_step(back_ring, 2)

    for p in range(NG // QB):
        packed[p * QB : (p + 1) * QB] = dot(pick[p], qkv[p * QB : p * QB + BAND]).astype(BF16)

    h_copy = lambda d, src: remote(sent.at[d], heads.at[src], s_h.at[d], r_h.at[src], d)

    def pack_head(d):
        block = outs[pl.ds(firsts[d], MOST), :]
        return jnp.concatenate([block[:HALF], block[HALF:]], axis=1).astype(BF16)

    def ship(d):
        sent[d] = pack_head(d)
        h_copy(d, me).start()

    corner = iota((QB, QB), 0) >= iota((QB, QB), 1)
    shipped = 0
    for p in range(NG // QB):
        upto = (p + 1) * QB
        query = packed[p * QB : upto, :HDIM] * jnp.asarray(HDIM**-0.5, BF16)
        scores = dot_nt(query, packed[:upto, HDIM : 2 * HDIM])
        edge = jnp.where(corner, scores[:, p * QB :], -jnp.inf)
        scores = edge if p == 0 else jnp.concatenate([scores[:, : p * QB], edge], axis=1)
        expo = jnp.exp(scores - jnp.max(scores, axis=1, keepdims=True))
        weight = 1.0 / jnp.sum(expo, axis=1, keepdims=True)
        outs[p * QB : upto] = dot(expo.astype(BF16), packed[:upto, 2 * HDIM :]) * weight
        if upto < NG:
            for d in range(shipped, upto // MOST):
                pl.when(me != d)(functools.partial(ship, d))
            shipped = upto // MOST
    for k in FAR_FIRST:
        d = lax.rem(me + k, N)
        pl.when(d >= shipped)(functools.partial(ship, d))
    heads[me] = pack_head(me)

    for step in (3, 4):
        ring_step(back_ring, step)
    for step in range(RING // 2 + 1):
        ring_sibling_wait(back_ring, step)

    others(lambda d: h_copy(d, d).wait_recv())
    left = iota((HALF, 128), 1) < HDIM
    tops, bottoms = [], []
    for h in range(0, N, 2):
        a, b = heads[h].astype(F32), heads[h + 1].astype(F32)
        tops.append(jnp.where(left, a, pltpu.roll(b, HDIM, 1)).astype(BF16))
        bottoms.append(jnp.where(left, pltpu.roll(a, HDIM, 1), b).astype(BF16))
    joined = jnp.concatenate([jnp.concatenate(tops, axis=1), jnp.concatenate(bottoms, axis=1)], axis=0)
    back = dot(joined, backs[...].reshape(N * HDIM, D))
    high, lower = two_terms(back)
    put = place[...]
    out[...] = (hidden[...].astype(F32) + dot_tn(put, high) + dot_tn(put, lower)).astype(BF16)

    others(lambda d: tot_copy(d, me).wait_send())
    others(lambda d: p_copy(d, me).wait_send())
    others(lambda d: s_copy(d, me).wait_send())
    others(lambda d: h_copy(d, me).wait_send())
    ring_done(back_ring)
    ring_done(row_ring)


def shards(tokens, group_pos, log_decay, in_weight, norm_gain, out_weight, inner_gain, qkv_weight, attn_out):
    vmem = pl.BlockSpec(memory_space=pltpu.VMEM)
    hbm = pl.BlockSpec(memory_space=pltpu.HBM)
    dma = pltpu.SemaphoreType.DMA
    return pl.pallas_call(
        layer,
        out_shape=jax.ShapeDtypeStruct((TOK, D), BF16),
        in_specs=[hbm] * 9,
        out_specs=vmem,
        scratch_shapes=[
            pltpu.VMEM((TOK, D), BF16),
            pltpu.VMEM((8, NG // 8), jnp.int32),
            pltpu.VMEM((HEADS, TOK), F32),
            pltpu.VMEM((D, W_IN), BF16),
            pltpu.VMEM((1, E), F32),
            pltpu.VMEM((E, D), BF16),
            pltpu.VMEM((1, D), F32),
            pltpu.VMEM((3 * HDIM, D), BF16),
            pltpu.VMEM((N, 1, 128), F32),
            pltpu.VMEM((N, 16, 256), BF16),
            pltpu.VMEM((N, 16, 256), BF16),
            pltpu.VMEM((N, 16, 256), BF16),
            pltpu.VMEM((N, 16, 256), BF16),
            pltpu.VMEM((TOK, W_IN), BF16),
            pltpu.VMEM((TOK, E), BF16),
            pltpu.VMEM((TOK, E), F32),
            pltpu.VMEM((TOK, E), F32),
            pltpu.VMEM((TOK, D), BF16),
            pltpu.VMEM((MOST, TOK), BF16),
            pltpu.VMEM((N, MOST, D), BF16),
            pltpu.VMEM((N, HDIM, D), BF16),
            pltpu.VMEM((N * MOST, 3 * HDIM), BF16),
            pltpu.VMEM((NG, 3 * HDIM), BF16),
            pltpu.VMEM((NG // QB, QB, BAND), BF16),
            pltpu.VMEM((NG + MOST, HDIM), F32),
            pltpu.SMEM((N,), jnp.int32),
            pltpu.VMEM((N, HALF, 128), BF16),
            pltpu.VMEM((N, HALF, 128), BF16),
        ]
        + [dma((11,))]
        + [dma((N,))] * 6
        + [dma((RING * PARTS,)), dma((N * PARTS,)), dma((RING,)), dma((RING,))] * 2
        + [dma((N,))] * 2,
        compiler_params=pltpu.CompilerParams(
            collective_id=0, has_side_effects=True, vmem_limit_bytes=60 * 2**20
        ),
    )(
        tokens,
        group_pos.reshape(8, NG // 8),
        log_decay.T,
        in_weight,
        norm_gain.reshape(1, E),
        out_weight,
        inner_gain.reshape(1, D),
        qkv_weight.transpose(0, 2, 1),
        attn_out,
    )


def solution(mesh):
    return jax.shard_map(
        shards,
        mesh=mesh,
        in_specs=(
            P(("grp", "seq"), None),
            P("grp"),
            P(("grp", "seq"), None),
            P(),
            P(),
            P(),
            P(),
            P("seq", None, None),
            P("seq", None, None),
        ),
        out_specs=P(("grp", "seq"), None),
        check_vma=False,
    )
```

```python
import functools

import jax
import jax.numpy as jnp
from jax import lax
from jax.experimental import pallas as pl
from jax.experimental.pallas import tpu as pltpu
from jax.sharding import PartitionSpec as P

MESH = pl.DeviceIdType.MESH
F32 = jnp.float32
BF16 = jnp.bfloat16

N = 16
RING = 8
TOK = 256
SUB = 128
D = 512
E = 1024
HEADS = 16
HDIM = 64
NST = 64
NG = 1024
MOST = 128
HALF = MOST // 2
W_IN = 2 * E + 2 * NST
PARTS = 4
QB = 512
BAND = QB + NG


FAR_FIRST = sorted(range(1, N), key=lambda k: -min(k, N - k))


def dot(a, b):
    return jnp.dot(a, b, preferred_element_type=F32)


def dot_nt(a, b):
    return lax.dot_general(a, b, (((1,), (1,)), ((), ())), preferred_element_type=F32)


def dot_tn(a, b):
    return lax.dot_general(a, b, (((0,), (0,)), ((), ())), preferred_element_type=F32)


def iota(shape, dim):
    return lax.broadcasted_iota(jnp.int32, shape, dim)


def two_terms(x):
    high = x.astype(BF16)
    return high, (x - high.astype(F32)).astype(BF16)


def spread(x, table):
    high, low = two_terms(x)
    return dot(high, table) + dot(low, table)


def layer(
    tokens_h,
    gpos_h,
    decay_h,
    w_in_h,
    gain_h,
    w_out_h,
    inner_h,
    w_qkv_h,
    w_back_h,
    out,
    tokens,
    gpos,
    decay,
    w_in,
    gain,
    w_out,
    inner,
    w_qkv,
    total,
    pieces,
    arrived,
    states,
    state_in,
    proj,
    xs,
    inner_y,
    factor,
    hidden,
    place,
    put,
    rows,
    backs,
    qkv,
    packed,
    pick,
    outs,
    firsts,
    sent,
    heads,
    loaded,
    s_tot,
    r_tot,
    s_p,
    r_p,
    s_s,
    r_s,
    s_g,
    r_g,
    s_gs,
    r_gs,
    s_w,
    r_w,
    s_ws,
    r_ws,
    s_h,
    r_h,
):
    me = lax.axis_index("seq")
    chip = me // 2
    core = lax.rem(me, 2)
    sibling = chip * 2 + (1 - core)

    def on_ring(step):
        return lax.rem(chip + step + RING, RING) * 2 + core

    def remote(src, dst, s_sem, r_sem, to):
        return pltpu.make_async_remote_copy(
            src_ref=src,
            dst_ref=dst,
            send_sem=s_sem,
            recv_sem=r_sem,
            device_id={"seq": to},
            device_id_type=MESH,
        )

    def others(body):
        for k in FAR_FIRST:
            body(lax.rem(me + k, N))

    wide = [pl.ds(0, E), pl.ds(2 * E, 2 * NST), pl.ds(E, E)]
    load = {
        name: pltpu.make_async_copy(src, dst, loaded.at[k])
        for k, (name, src, dst) in enumerate(
            (
                ("decay", decay_h, decay),
                ("tokens", tokens_h, tokens),
                *((c, w_in_h.at[:, cols], w_in.at[:, cols]) for c, cols in enumerate(wide)),
                ("back", w_back_h.at[0], backs.at[me]),
                ("gpos", gpos_h, gpos),
                ("gain", gain_h, gain),
                ("out", w_out_h, w_out),
                ("inner", inner_h, inner),
                ("qkv", w_qkv_h.at[0], w_qkv),
            )
        )
    }
    late = (2, "gpos", "gain", "out", "inner", "qkv")
    for name, copy in load.items():
        if name not in late:
            copy.start()
    barrier = pltpu.get_barrier_semaphore()
    others(lambda d: pl.semaphore_signal(barrier, inc=1, device_id={"seq": d}, device_id_type=MESH))

    load["decay"].wait()
    ld = decay[...]
    tri = (iota((TOK, TOK), 0) >= iota((TOK, TOK), 1)).astype(BF16)
    first, rest = two_terms(ld)
    second, third = two_terms(ld - first.astype(F32))
    cum = dot_nt(tri, first) + dot_nt(tri, second) + dot_nt(tri, third)
    end = cum[TOK - 1 : TOK]
    total[me] = jnp.pad(end, ((0, 0), (0, 128 - HEADS)))

    tot_copy = lambda d, src: remote(total.at[src], total.at[src], s_tot.at[d], r_tot.at[src], d)

    def ring_copy(ring, block, part, way, hops, slot):
        buf, parts, s_sem, r_sem, _, _ = ring
        size = buf.shape[1] // parts
        ref = buf.at[block, pl.ds(part * size, size), :]
        return remote(ref, ref, s_sem.at[slot], r_sem.at[parts * block + part], on_ring(hops * way))

    def ring_near(parts, part, way):
        return (part < parts // 2) == (way == 1)

    def ring_sends(ring, step):
        parts = ring[1]
        for part in range(parts):
            for way in (1, -1):
                block = on_ring(-way * step)
                slot = part * 2 + (way + 1) // 2
                copies = [ring_copy(ring, block, part, way, 1, 2 * parts * step + slot)]
                if step == 2 and ring_near(parts, part, way):
                    copies.insert(0, ring_copy(ring, block, part, way, 2, 6 * parts + slot))
                yield part, way, copies

    def ring_wait(ring, step, part, way):
        ring_copy(ring, on_ring(-way * step), part, way, 1, 0).wait_recv()

    def ring_hand(ring, block):
        buf, _, _, _, s_sib, r_sib = ring
        return remote(buf.at[block], buf.at[block], s_sib.at[block // 2], r_sib.at[block // 2], sibling)

    def ring_ways(step):
        return (1, -1) if 0 < step < RING // 2 else (1,)

    def ring_step(ring, step):
        parts = ring[1]
        if step <= 2:
            for part, way, copies in ring_sends(ring, step):
                if step > 0:
                    ring_wait(ring, step, part, way)
                for copy in copies:
                    copy.start()
        else:
            for part in range(parts):
                for way in (1, -1):
                    if step == 3 or ring_near(parts, part, way):
                        ring_wait(ring, step, part, way)
        for way in ring_ways(step):
            ring_hand(ring, on_ring(-way * step)).start()

    def ring_sibling_wait(ring, step):
        for way in ring_ways(step):
            ring_hand(ring, (on_ring(-way * step) // 2) * 2 + 1 - core).wait_recv()

    def ring_done(ring):
        for step in range(3):
            for _, _, copies in ring_sends(ring, step):
                for copy in copies:
                    copy.wait_send()
        for b in range(RING):
            ring_hand(ring, b * 2 + core).wait_send()

    back_ring = (backs, 2, s_w, r_w, s_ws, r_ws)
    row_ring = (rows, PARTS, s_g, r_g, s_gs, r_gs)

    load["tokens"].wait()
    toks = tokens[...]

    def project_in(c):
        load[c].wait()
        proj[:, wide[c]] = dot(toks, w_in[:, wide[c]]).astype(BF16)

    project_in(0)
    project_in(1)
    for name in late:
        load[name].start()

    mids = [cum[SUB // 2 - 1 : SUB // 2], cum[SUB + SUB // 2 - 1 : SUB + SUB // 2]]
    rel = jnp.concatenate([cum[:SUB] - mids[0], cum[SUB:] - mids[1]], axis=0)
    table = (iota((HEADS, E), 1) // HDIM == iota((HEADS, E), 0)).astype(BF16)
    f_in = spread(jnp.exp(rel), table)
    f_out = spread(jnp.exp(-rel), table)
    few = jnp.concatenate(
        [mids[0], mids[1], end - mids[0], end - mids[1], mids[1] - mids[0], end, end, end], axis=0
    )
    few = spread(jnp.exp(few), table)
    xs[...] = (proj[:, :E].astype(F32) * f_out).astype(BF16)
    bc = proj[:, 2 * E :]
    bmat, cmat = bc[:, :NST], bc[:, NST:]
    low = iota((SUB, SUB), 0) >= iota((SUB, SUB), 1)
    u = [dot_tn(bmat[k * SUB : (k + 1) * SUB], xs[k * SUB : (k + 1) * SUB]) for k in range(2)]
    local = (u[0] * few[2:3] + u[1] * few[3:4]).astype(BF16)
    for d in range(N):
        r, c = 16 * (d // 4), 256 * (d % 4)
        pieces[d] = local[r : r + 16, c : c + 256]

    p_copy = lambda d, src: remote(pieces.at[d], arrived.at[src], s_p.at[d], r_p.at[src], d)
    pl.semaphore_wait(barrier, N - 1)
    others(lambda d: tot_copy(d, me).start())
    others(lambda d: p_copy(d, me).start())
    load["back"].wait()
    ring_step(back_ring, 0)
    arrived[me] = pieces[me]

    load["gpos"].wait()
    gp = gpos[...]
    base = me * TOK
    before = [jnp.sum((gp < d * TOK).astype(jnp.int32)) for d in range(N)] + [jnp.int32(NG)]
    for d in range(N):
        firsts[d] = before[d]
    here = firsts[me]
    at = base + iota((TOK, 128), 0)
    less = jnp.zeros((TOK, 128), F32)
    same = jnp.zeros((TOK, 128), F32)
    for r in range(8):
        row = gp[r : r + 1]
        less = less + (row < at).astype(F32)
        same = same + (row == at).astype(F32)
    ones = jnp.ones((8, 128), BF16)
    rank = dot_nt(ones, less.astype(BF16))[0:1] - here.astype(F32)
    start = dot_nt(ones, same.astype(BF16))[0:1]
    one_hot = jnp.where((rank == iota((MOST, TOK), 0).astype(F32)) & (start > 0.5), 1.0, 0.0)
    place[...] = one_hot.astype(BF16)
    back_to = one_hot.T.astype(BF16)
    put[...] = jnp.concatenate([back_to, back_to], axis=1)

    u0 = (u[0] * few[4:5]).astype(BF16)
    for k in range(2):
        b_k, c_k = bmat[k * SUB : (k + 1) * SUB], cmat[k * SUB : (k + 1) * SUB]
        g = jnp.where(low, dot_nt(c_k, b_k), 0.0).astype(BF16)
        y = dot(g, xs[k * SUB : (k + 1) * SUB])
        if k == 1:
            y = y + dot(c_k, u0)
        inner_y[k * SUB : (k + 1) * SUB] = y
    project_in(2)
    gate = proj[:, E : 2 * E].astype(F32)
    factor[...] = f_in * (gate / (1.0 + jnp.exp(-gate)))

    others(lambda d: tot_copy(d, d).wait_recv())
    lanes = iota((128, 256), 1) // HDIM + 4 * lax.rem(me, 4)
    mine = (lanes == iota((128, 256), 0)).astype(BF16)
    sums = jnp.concatenate([total[d] for d in range(N)], axis=0)
    fades = spread(jnp.exp(sums), mine)

    others(lambda d: p_copy(d, d).wait_recv())
    run = jnp.zeros((16, 256), F32)
    for d in range(N):
        states[d] = run.astype(BF16)
        run = run * fades[d : d + 1] + arrived[d].astype(F32)
    s_copy = lambda d, src: remote(states.at[d], state_in.at[src], s_s.at[d], r_s.at[src], d)
    others(lambda d: s_copy(d, me).start())
    state_in[me] = states[me]

    others(lambda d: s_copy(d, d).wait_recv())
    ring_step(back_ring, 1)

    squares = jnp.zeros((TOK, 1), F32)
    for q in range(4):
        cols = slice(256 * q, 256 * q + 256)
        s = jnp.concatenate([state_in[4 * k + q] for k in range(4)], axis=0).astype(F32)
        s = [(s * few[k : k + 1, cols]).astype(BF16) for k in range(2)]
        carried = jnp.concatenate([dot(cmat[k * SUB : (k + 1) * SUB], s[k]) for k in range(2)], axis=0)
        gated = (inner_y[:, cols] + carried) * factor[:, cols]
        inner_y[:, cols] = gated
        squares = squares + jnp.sum(gated * gated, axis=1, keepdims=True)
    for name in ("gain", "out", "inner", "qkv"):
        load[name].wait()
    scale = lax.rsqrt(squares * (1.0 / E) + 1e-5)
    normed = (inner_y[...] * scale * gain[...]).astype(BF16)
    hid = (toks.astype(F32) + dot(normed, w_out[...])).astype(BF16)
    hidden[...] = hid
    own = dot(place[...], hid)
    own = own * lax.rsqrt(jnp.mean(own * own, axis=1, keepdims=True) + 1e-5) * inner[...]
    rows[me] = own.astype(BF16)

    ring_step(row_ring, 0)

    lane = iota((1, MOST), 1)
    slots = [jnp.where(lane + before[d] < before[d + 1], lane + before[d], -1) for d in range(N)]
    for p in range(NG // QB):
        for t in range(BAND // MOST):
            d = p * QB // MOST + t
            want = iota((QB, MOST), 0) + p * QB
            pick[p, :, t * MOST : (t + 1) * MOST] = (want == slots[d]).astype(BF16)
    outs[...] = jnp.zeros_like(outs)

    def project(block):
        qkv[pl.ds(pl.multiple_of(block * MOST, MOST), MOST), :] = dot_nt(rows[block], w_qkv[...]).astype(BF16)

    project(me)
    for step in range(1, RING // 2 + 1):
        ring_step(row_ring, step)
        ring_sibling_wait(row_ring, step - 1)
        for way in ring_ways(step - 1):
            project((on_ring(-way * (step - 1)) // 2) * 2 + 1 - core)
        for way in ring_ways(step):
            project(on_ring(-way * step))
    ring_sibling_wait(row_ring, RING // 2)
    project((on_ring(RING // 2) // 2) * 2 + 1 - core)
    ring_step(back_ring, 2)

    for p in range(NG // QB):
        packed[p * QB : (p + 1) * QB] = dot(pick[p], qkv[p * QB : p * QB + BAND]).astype(BF16)

    h_copy = lambda d, src: remote(sent.at[d], heads.at[src], s_h.at[d], r_h.at[src], d)

    def pack_head(d):
        block = outs[pl.ds(firsts[d], MOST), :]
        return jnp.concatenate([block[:HALF], block[HALF:]], axis=1).astype(BF16)

    def ship(d):
        sent[d] = pack_head(d)
        h_copy(d, me).start()

    corner = iota((QB, QB), 0) >= iota((QB, QB), 1)
    shipped = 0
    for p in range(NG // QB):
        upto = (p + 1) * QB
        query = packed[p * QB : upto, :HDIM] * jnp.asarray(HDIM**-0.5, BF16)
        scores = dot_nt(query, packed[:upto, HDIM : 2 * HDIM])
        edge = jnp.where(corner, scores[:, p * QB :], -jnp.inf)
        scores = edge if p == 0 else jnp.concatenate([scores[:, : p * QB], edge], axis=1)
        expo = jnp.exp(scores - jnp.max(scores, axis=1, keepdims=True))
        weight = 1.0 / jnp.sum(expo, axis=1, keepdims=True)
        outs[p * QB : upto] = dot(expo.astype(BF16), packed[:upto, 2 * HDIM :]) * weight
        if upto < NG:
            for d in range(shipped, upto // MOST):
                pl.when(me != d)(functools.partial(ship, d))
            shipped = upto // MOST
    for k in FAR_FIRST:
        d = lax.rem(me + k, N)
        pl.when(d >= shipped)(functools.partial(ship, d))
    heads[me] = pack_head(me)

    for step in (3, 4):
        ring_step(back_ring, step)
    for step in range(RING // 2 + 1):
        ring_sibling_wait(back_ring, step)

    others(lambda d: h_copy(d, d).wait_recv())
    left = iota((HALF, 128), 1) < HDIM
    tops, bottoms = [], []
    for h in range(0, N, 2):
        a, b = heads[h].astype(F32), heads[h + 1].astype(F32)
        tops.append(jnp.where(left, a, pltpu.roll(b, HDIM, 1)).astype(BF16))
        bottoms.append(jnp.where(left, pltpu.roll(a, HDIM, 1), b).astype(BF16))
    joined = jnp.concatenate([jnp.concatenate(tops, axis=1), jnp.concatenate(bottoms, axis=1)], axis=0)
    back = dot(joined, backs[...].reshape(N * HDIM, D))
    placed = dot(put[...], jnp.concatenate(two_terms(back), axis=0))
    out[...] = (hidden[...].astype(F32) + placed).astype(BF16)

    others(lambda d: tot_copy(d, me).wait_send())
    others(lambda d: p_copy(d, me).wait_send())
    others(lambda d: s_copy(d, me).wait_send())
    others(lambda d: h_copy(d, me).wait_send())
    ring_done(back_ring)
    ring_done(row_ring)


def shards(tokens, group_pos, log_decay, in_weight, norm_gain, out_weight, inner_gain, qkv_weight, attn_out):
    vmem = pl.BlockSpec(memory_space=pltpu.VMEM)
    hbm = pl.BlockSpec(memory_space=pltpu.HBM)
    dma = pltpu.SemaphoreType.DMA
    return pl.pallas_call(
        layer,
        out_shape=jax.ShapeDtypeStruct((TOK, D), BF16),
        in_specs=[hbm] * 9,
        out_specs=vmem,
        scratch_shapes=[
            pltpu.VMEM((TOK, D), BF16),
            pltpu.VMEM((8, NG // 8), jnp.int32),
            pltpu.VMEM((HEADS, TOK), F32),
            pltpu.VMEM((D, W_IN), BF16),
            pltpu.VMEM((1, E), F32),
            pltpu.VMEM((E, D), BF16),
            pltpu.VMEM((1, D), F32),
            pltpu.VMEM((3 * HDIM, D), BF16),
            pltpu.VMEM((N, 1, 128), F32),
            pltpu.VMEM((N, 16, 256), BF16),
            pltpu.VMEM((N, 16, 256), BF16),
            pltpu.VMEM((N, 16, 256), BF16),
            pltpu.VMEM((N, 16, 256), BF16),
            pltpu.VMEM((TOK, W_IN), BF16),
            pltpu.VMEM((TOK, E), BF16),
            pltpu.VMEM((TOK, E), F32),
            pltpu.VMEM((TOK, E), F32),
            pltpu.VMEM((TOK, D), BF16),
            pltpu.VMEM((MOST, TOK), BF16),
            pltpu.VMEM((TOK, 2 * MOST), BF16),
            pltpu.VMEM((N, MOST, D), BF16),
            pltpu.VMEM((N, HDIM, D), BF16),
            pltpu.VMEM((N * MOST, 3 * HDIM), BF16),
            pltpu.VMEM((NG, 3 * HDIM), BF16),
            pltpu.VMEM((NG // QB, QB, BAND), BF16),
            pltpu.VMEM((NG + MOST, HDIM), F32),
            pltpu.SMEM((N,), jnp.int32),
            pltpu.VMEM((N, HALF, 128), BF16),
            pltpu.VMEM((N, HALF, 128), BF16),
        ]
        + [dma((11,))]
        + [dma((N,))] * 6
        + [dma((RING * PARTS,)), dma((N * PARTS,)), dma((RING,)), dma((RING,))] * 2
        + [dma((N,))] * 2,
        compiler_params=pltpu.CompilerParams(
            collective_id=0, has_side_effects=True, vmem_limit_bytes=48 * 2**20
        ),
    )(
        *(
            pltpu.with_memory_space_constraint(x, pltpu.HBM)
            for x in (
                tokens,
                group_pos.reshape(8, NG // 8),
                log_decay.T,
                in_weight,
                norm_gain.reshape(1, E),
                out_weight,
                inner_gain.reshape(1, D),
                qkv_weight.transpose(0, 2, 1),
                attn_out,
            )
        )
    )


def solution(mesh):
    return jax.shard_map(
        shards,
        mesh=mesh,
        in_specs=(
            P(("grp", "seq"), None),
            P("grp"),
            P(("grp", "seq"), None),
            P(),
            P(),
            P(),
            P(),
            P("seq", None, None),
            P("seq", None, None),
        ),
        out_specs=P(("grp", "seq"), None),
        check_vma=False,
    )
```

```python
import functools

import jax
import jax.numpy as jnp
from jax import lax
from jax.experimental import pallas as pl
from jax.experimental.pallas import tpu as pltpu
from jax.sharding import PartitionSpec as P

MESH = pl.DeviceIdType.MESH
F32 = jnp.float32
BF16 = jnp.bfloat16

N = 16
RING = 8
TOK = 256
SUB = 128
D = 512
E = 1024
HEADS = 16
HDIM = 64
NST = 64
NG = 1024
MOST = 128
HALF = MOST // 2
W_IN = 2 * E + 2 * NST
PARTS = 4
QB = 512
BAND = QB + NG


FAR_FIRST = sorted(range(1, N), key=lambda k: -min(k, N - k))


def dot(a, b):
    return jnp.dot(a, b, preferred_element_type=F32)


def dot_nt(a, b):
    return lax.dot_general(a, b, (((1,), (1,)), ((), ())), preferred_element_type=F32)


def dot_tn(a, b):
    return lax.dot_general(a, b, (((0,), (0,)), ((), ())), preferred_element_type=F32)


def iota(shape, dim):
    return lax.broadcasted_iota(jnp.int32, shape, dim)


def two_terms(x):
    high = x.astype(BF16)
    return high, (x - high.astype(F32)).astype(BF16)


def spread(x, table):
    high, low = two_terms(x)
    return dot(high, table) + dot(low, table)


def layer(
    tokens_h,
    gpos_h,
    decay_h,
    w_in_h,
    gain_h,
    w_out_h,
    inner_h,
    w_qkv_h,
    w_back_h,
    out,
    tokens,
    gpos,
    decay,
    w_in,
    gain,
    w_out,
    inner,
    w_qkv,
    total,
    pieces,
    arrived,
    states,
    state_in,
    proj,
    xs,
    inner_y,
    factor,
    hidden,
    place,
    put,
    rows,
    backs,
    qkv,
    packed,
    pick,
    outs,
    firsts,
    sent,
    heads,
    loaded,
    s_tot,
    r_tot,
    s_p,
    r_p,
    s_s,
    r_s,
    s_g,
    r_g,
    s_gs,
    r_gs,
    s_w,
    r_w,
    s_ws,
    r_ws,
    s_h,
    r_h,
):
    me = lax.axis_index("seq")
    chip = me // 2
    core = lax.rem(me, 2)
    sibling = chip * 2 + (1 - core)

    def on_ring(step):
        return lax.rem(chip + step + RING, RING) * 2 + core

    def remote(src, dst, s_sem, r_sem, to):
        return pltpu.make_async_remote_copy(
            src_ref=src,
            dst_ref=dst,
            send_sem=s_sem,
            recv_sem=r_sem,
            device_id={"seq": to},
            device_id_type=MESH,
        )

    def others(body):
        for k in FAR_FIRST:
            body(lax.rem(me + k, N))

    wide = [pl.ds(0, E), pl.ds(2 * E, 2 * NST), pl.ds(E, E)]
    load = {
        name: pltpu.make_async_copy(src, dst, loaded.at[k])
        for k, (name, src, dst) in enumerate(
            (
                ("decay", decay_h, decay),
                ("tokens", tokens_h, tokens),
                *((c, w_in_h.at[:, cols], w_in.at[:, cols]) for c, cols in enumerate(wide)),
                ("back", w_back_h.at[0], backs.at[me]),
                ("gpos", gpos_h, gpos),
                ("gain", gain_h, gain),
                ("out", w_out_h, w_out),
                ("inner", inner_h, inner),
                ("qkv", w_qkv_h.at[0], w_qkv),
            )
        )
    }
    late = (2, "gpos", "gain", "out", "inner", "qkv")
    for name, copy in load.items():
        if name not in late:
            copy.start()
    barrier = pltpu.get_barrier_semaphore()
    others(lambda d: pl.semaphore_signal(barrier, inc=1, device_id={"seq": d}, device_id_type=MESH))

    load["decay"].wait()
    ld = decay[...]
    tri = (iota((TOK, TOK), 0) >= iota((TOK, TOK), 1)).astype(BF16)
    first, rest = two_terms(ld)
    second, third = two_terms(ld - first.astype(F32))
    cum = dot_nt(tri, first) + dot_nt(tri, second) + dot_nt(tri, third)
    end = cum[TOK - 1 : TOK]
    total[me] = jnp.pad(end, ((0, 0), (0, 128 - HEADS)))

    tot_copy = lambda d, src: remote(total.at[src], total.at[src], s_tot.at[d], r_tot.at[src], d)

    def ring_copy(ring, block, part, way, hops, slot):
        buf, parts, s_sem, r_sem, _, _ = ring
        size = buf.shape[1] // parts
        ref = buf.at[block, pl.ds(part * size, size), :]
        return remote(ref, ref, s_sem.at[slot], r_sem.at[parts * block + part], on_ring(hops * way))

    def ring_parts(parts, step):
        for order in range(parts if step < RING // 2 else parts // 2):
            for way in (1, -1):
                yield order, order if way == 1 else (order + parts // 2) % parts, way

    def ring_sends(ring, step):
        parts = ring[1]
        for order, part, way in ring_parts(parts, step):
            block = on_ring(-way * step)
            slot = part * 2 + (way + 1) // 2
            copies = []
            if step == 2 and parts // 4 <= order < parts // 2:
                copies.append(ring_copy(ring, block, part, way, 2, 6 * parts + slot))
            if step < 3 or (step == 3 and order < parts // 4):
                copies.append(ring_copy(ring, block, part, way, 1, 2 * parts * step + slot))
            yield part, way, copies

    def ring_wait(ring, step, part, way):
        ring_copy(ring, on_ring(-way * step), part, way, 1, 0).wait_recv()

    def ring_hand(ring, block):
        buf, _, _, _, s_sib, r_sib = ring
        return remote(buf.at[block], buf.at[block], s_sib.at[block // 2], r_sib.at[block // 2], sibling)

    def ring_ways(step):
        return (1, -1) if 0 < step < RING // 2 else (1,)

    def ring_step(ring, step):
        for part, way, copies in ring_sends(ring, step):
            if step > 0:
                ring_wait(ring, step, part, way)
            for copy in copies:
                copy.start()
        for way in ring_ways(step):
            ring_hand(ring, on_ring(-way * step)).start()

    def ring_sibling_wait(ring, step):
        for way in ring_ways(step):
            ring_hand(ring, (on_ring(-way * step) // 2) * 2 + 1 - core).wait_recv()

    def ring_done(ring):
        for step in range(RING // 2):
            for _, _, copies in ring_sends(ring, step):
                for copy in copies:
                    copy.wait_send()
        for b in range(RING):
            ring_hand(ring, b * 2 + core).wait_send()

    back_ring = (backs, 2, s_w, r_w, s_ws, r_ws)
    row_ring = (rows, PARTS, s_g, r_g, s_gs, r_gs)

    load["tokens"].wait()
    toks = tokens[...]

    def project_in(c):
        load[c].wait()
        proj[:, wide[c]] = dot(toks, w_in[:, wide[c]]).astype(BF16)

    project_in(0)
    project_in(1)
    for name in late:
        load[name].start()

    mids = [cum[SUB // 2 - 1 : SUB // 2], cum[SUB + SUB // 2 - 1 : SUB + SUB // 2]]
    rel = jnp.concatenate([cum[:SUB] - mids[0], cum[SUB:] - mids[1]], axis=0)
    table = (iota((HEADS, E), 1) // HDIM == iota((HEADS, E), 0)).astype(BF16)
    f_in = spread(jnp.exp(rel), table)
    f_out = spread(jnp.exp(-rel), table)
    few = jnp.concatenate(
        [mids[0], mids[1], end - mids[0], end - mids[1], mids[1] - mids[0], end, end, end], axis=0
    )
    few = spread(jnp.exp(few), table)
    xs[...] = (proj[:, :E].astype(F32) * f_out).astype(BF16)
    bc = proj[:, 2 * E :]
    bmat, cmat = bc[:, :NST], bc[:, NST:]
    low = iota((SUB, SUB), 0) >= iota((SUB, SUB), 1)
    u = [dot_tn(bmat[k * SUB : (k + 1) * SUB], xs[k * SUB : (k + 1) * SUB]) for k in range(2)]
    local = (u[0] * few[2:3] + u[1] * few[3:4]).astype(BF16)
    for d in range(N):
        r, c = 16 * (d // 4), 256 * (d % 4)
        pieces[d] = local[r : r + 16, c : c + 256]

    p_copy = lambda d, src: remote(pieces.at[d], arrived.at[src], s_p.at[d], r_p.at[src], d)
    pl.semaphore_wait(barrier, N - 1)
    others(lambda d: tot_copy(d, me).start())
    others(lambda d: p_copy(d, me).start())
    load["back"].wait()
    ring_step(back_ring, 0)
    arrived[me] = pieces[me]

    load["gpos"].wait()
    gp = gpos[...]
    base = me * TOK
    before = [jnp.sum((gp < d * TOK).astype(jnp.int32)) for d in range(N)] + [jnp.int32(NG)]
    for d in range(N):
        firsts[d] = before[d]
    here = firsts[me]
    at = base + iota((TOK, 128), 0)
    less = jnp.zeros((TOK, 128), F32)
    same = jnp.zeros((TOK, 128), F32)
    for r in range(8):
        row = gp[r : r + 1]
        less = less + (row < at).astype(F32)
        same = same + (row == at).astype(F32)
    ones = jnp.ones((8, 128), BF16)
    rank = dot_nt(ones, less.astype(BF16))[0:1] - here.astype(F32)
    start = dot_nt(ones, same.astype(BF16))[0:1]
    one_hot = jnp.where((rank == iota((MOST, TOK), 0).astype(F32)) & (start > 0.5), 1.0, 0.0)
    place[...] = one_hot.astype(BF16)
    back_to = one_hot.T.astype(BF16)
    put[...] = jnp.concatenate([back_to, back_to], axis=1)

    u0 = (u[0] * few[4:5]).astype(BF16)
    for k in range(2):
        b_k, c_k = bmat[k * SUB : (k + 1) * SUB], cmat[k * SUB : (k + 1) * SUB]
        g = jnp.where(low, dot_nt(c_k, b_k), 0.0).astype(BF16)
        y = dot(g, xs[k * SUB : (k + 1) * SUB])
        if k == 1:
            y = y + dot(c_k, u0)
        inner_y[k * SUB : (k + 1) * SUB] = y
    project_in(2)
    gate = proj[:, E : 2 * E].astype(F32)
    factor[...] = f_in * (gate / (1.0 + jnp.exp(-gate)))

    others(lambda d: tot_copy(d, d).wait_recv())
    lanes = iota((128, 256), 1) // HDIM + 4 * lax.rem(me, 4)
    mine = (lanes == iota((128, 256), 0)).astype(BF16)
    sums = jnp.concatenate([total[d] for d in range(N)], axis=0)
    fades = spread(jnp.exp(sums), mine)

    others(lambda d: p_copy(d, d).wait_recv())
    run = jnp.zeros((16, 256), F32)
    for d in range(N):
        states[d] = run.astype(BF16)
        run = run * fades[d : d + 1] + arrived[d].astype(F32)
    s_copy = lambda d, src: remote(states.at[d], state_in.at[src], s_s.at[d], r_s.at[src], d)
    others(lambda d: s_copy(d, me).start())
    state_in[me] = states[me]

    others(lambda d: s_copy(d, d).wait_recv())
    ring_step(back_ring, 1)

    squares = jnp.zeros((TOK, 1), F32)
    for q in range(4):
        cols = slice(256 * q, 256 * q + 256)
        s = jnp.concatenate([state_in[4 * k + q] for k in range(4)], axis=0).astype(F32)
        s = [(s * few[k : k + 1, cols]).astype(BF16) for k in range(2)]
        carried = jnp.concatenate([dot(cmat[k * SUB : (k + 1) * SUB], s[k]) for k in range(2)], axis=0)
        gated = (inner_y[:, cols] + carried) * factor[:, cols]
        inner_y[:, cols] = gated
        squares = squares + jnp.sum(gated * gated, axis=1, keepdims=True)
    for name in ("gain", "out", "inner", "qkv"):
        load[name].wait()
    scale = lax.rsqrt(squares * (1.0 / E) + 1e-5)
    normed = (inner_y[...] * scale * gain[...]).astype(BF16)
    hid = (toks.astype(F32) + dot(normed, w_out[...])).astype(BF16)
    hidden[...] = hid
    own = dot(place[...], hid)
    own = own * lax.rsqrt(jnp.mean(own * own, axis=1, keepdims=True) + 1e-5) * inner[...]
    rows[me] = own.astype(BF16)

    ring_step(row_ring, 0)

    lane = iota((1, MOST), 1)
    slots = [jnp.where(lane + before[d] < before[d + 1], lane + before[d], -1) for d in range(N)]
    for p in range(NG // QB):
        for t in range(BAND // MOST):
            d = p * QB // MOST + t
            want = iota((QB, MOST), 0) + p * QB
            pick[p, :, t * MOST : (t + 1) * MOST] = (want == slots[d]).astype(BF16)
    outs[...] = jnp.zeros_like(outs)

    def project(block):
        qkv[pl.ds(pl.multiple_of(block * MOST, MOST), MOST), :] = dot_nt(rows[block], w_qkv[...]).astype(BF16)

    project(me)
    for step in range(1, RING // 2 + 1):
        ring_step(row_ring, step)
        if step == 4:
            ring_step(back_ring, 2)
        ring_sibling_wait(row_ring, step - 1)
        for way in ring_ways(step - 1):
            project((on_ring(-way * (step - 1)) // 2) * 2 + 1 - core)
        for way in ring_ways(step):
            project(on_ring(-way * step))
    ring_sibling_wait(row_ring, RING // 2)
    project((on_ring(RING // 2) // 2) * 2 + 1 - core)

    for p in range(NG // QB):
        packed[p * QB : (p + 1) * QB] = dot(pick[p], qkv[p * QB : p * QB + BAND]).astype(BF16)

    h_copy = lambda d, src: remote(sent.at[d], heads.at[src], s_h.at[d], r_h.at[src], d)

    def pack_head(d):
        block = outs[pl.ds(firsts[d], MOST), :]
        return jnp.concatenate([block[:HALF], block[HALF:]], axis=1).astype(BF16)

    def ship(d):
        sent[d] = pack_head(d)
        h_copy(d, me).start()

    corner = iota((QB, QB), 0) >= iota((QB, QB), 1)
    shipped = 0
    for p in range(NG // QB):
        upto = (p + 1) * QB
        query = packed[p * QB : upto, :HDIM] * jnp.asarray(HDIM**-0.5, BF16)
        scores = dot_nt(query, packed[:upto, HDIM : 2 * HDIM])
        edge = jnp.where(corner, scores[:, p * QB :], -jnp.inf)
        scores = edge if p == 0 else jnp.concatenate([scores[:, : p * QB], edge], axis=1)
        expo = jnp.exp(scores - jnp.max(scores, axis=1, keepdims=True))
        weight = 1.0 / jnp.sum(expo, axis=1, keepdims=True)
        outs[p * QB : upto] = dot(expo.astype(BF16), packed[:upto, 2 * HDIM :]) * weight
        if upto < NG:
            for d in range(shipped, upto // MOST):
                pl.when(me != d)(functools.partial(ship, d))
            shipped = upto // MOST
    for k in FAR_FIRST:
        d = lax.rem(me + k, N)
        pl.when(d >= shipped)(functools.partial(ship, d))
    heads[me] = pack_head(me)

    for step in (3, 4):
        ring_step(back_ring, step)
    for step in range(RING // 2 + 1):
        ring_sibling_wait(back_ring, step)

    others(lambda d: h_copy(d, d).wait_recv())
    left = iota((HALF, 128), 1) < HDIM
    tops, bottoms = [], []
    for h in range(0, N, 2):
        a, b = heads[h].astype(F32), heads[h + 1].astype(F32)
        tops.append(jnp.where(left, a, pltpu.roll(b, HDIM, 1)).astype(BF16))
        bottoms.append(jnp.where(left, pltpu.roll(a, HDIM, 1), b).astype(BF16))
    joined = jnp.concatenate([jnp.concatenate(tops, axis=1), jnp.concatenate(bottoms, axis=1)], axis=0)
    back = dot(joined, backs[...].reshape(N * HDIM, D))
    placed = dot(put[...], jnp.concatenate(two_terms(back), axis=0))
    out[...] = (hidden[...].astype(F32) + placed).astype(BF16)

    others(lambda d: tot_copy(d, me).wait_send())
    others(lambda d: p_copy(d, me).wait_send())
    others(lambda d: s_copy(d, me).wait_send())
    others(lambda d: h_copy(d, me).wait_send())
    ring_done(back_ring)
    ring_done(row_ring)


def shards(tokens, group_pos, log_decay, in_weight, norm_gain, out_weight, inner_gain, qkv_weight, attn_out):
    vmem = pl.BlockSpec(memory_space=pltpu.VMEM)
    hbm = pl.BlockSpec(memory_space=pltpu.HBM)
    dma = pltpu.SemaphoreType.DMA
    return pl.pallas_call(
        layer,
        out_shape=jax.ShapeDtypeStruct((TOK, D), BF16),
        in_specs=[hbm] * 9,
        out_specs=vmem,
        scratch_shapes=[
            pltpu.VMEM((TOK, D), BF16),
            pltpu.VMEM((8, NG // 8), jnp.int32),
            pltpu.VMEM((HEADS, TOK), F32),
            pltpu.VMEM((D, W_IN), BF16),
            pltpu.VMEM((1, E), F32),
            pltpu.VMEM((E, D), BF16),
            pltpu.VMEM((1, D), F32),
            pltpu.VMEM((3 * HDIM, D), BF16),
            pltpu.VMEM((N, 1, 128), F32),
            pltpu.VMEM((N, 16, 256), BF16),
            pltpu.VMEM((N, 16, 256), BF16),
            pltpu.VMEM((N, 16, 256), BF16),
            pltpu.VMEM((N, 16, 256), BF16),
            pltpu.VMEM((TOK, W_IN), BF16),
            pltpu.VMEM((TOK, E), BF16),
            pltpu.VMEM((TOK, E), F32),
            pltpu.VMEM((TOK, E), F32),
            pltpu.VMEM((TOK, D), BF16),
            pltpu.VMEM((MOST, TOK), BF16),
            pltpu.VMEM((TOK, 2 * MOST), BF16),
            pltpu.VMEM((N, MOST, D), BF16),
            pltpu.VMEM((N, HDIM, D), BF16),
            pltpu.VMEM((N * MOST, 3 * HDIM), BF16),
            pltpu.VMEM((NG, 3 * HDIM), BF16),
            pltpu.VMEM((NG // QB, QB, BAND), BF16),
            pltpu.VMEM((NG + MOST, HDIM), F32),
            pltpu.SMEM((N,), jnp.int32),
            pltpu.VMEM((N, HALF, 128), BF16),
            pltpu.VMEM((N, HALF, 128), BF16),
        ]
        + [dma((11,))]
        + [dma((N,))] * 6
        + [dma((RING * PARTS,)), dma((N * PARTS,)), dma((RING,)), dma((RING,))] * 2
        + [dma((N,))] * 2,
        compiler_params=pltpu.CompilerParams(
            collective_id=0, has_side_effects=True, vmem_limit_bytes=48 * 2**20
        ),
    )(
        *(
            pltpu.with_memory_space_constraint(x, pltpu.HBM)
            for x in (
                tokens,
                group_pos.reshape(8, NG // 8),
                log_decay.T,
                in_weight,
                norm_gain.reshape(1, E),
                out_weight,
                inner_gain.reshape(1, D),
                qkv_weight.transpose(0, 2, 1),
                attn_out,
            )
        )
    )


def solution(mesh):
    return jax.shard_map(
        shards,
        mesh=mesh,
        in_specs=(
            P(("grp", "seq"), None),
            P("grp"),
            P(("grp", "seq"), None),
            P(),
            P(),
            P(),
            P(),
            P("seq", None, None),
            P("seq", None, None),
        ),
        out_specs=P(("grp", "seq"), None),
        check_vma=False,
    )
```

```python
import functools

import jax
import jax.numpy as jnp
from jax import lax
from jax.experimental import pallas as pl
from jax.experimental.pallas import tpu as pltpu
from jax.sharding import PartitionSpec as P

MESH = pl.DeviceIdType.MESH
F32 = jnp.float32
BF16 = jnp.bfloat16

N = 16
RING = 8
TOK = 256
SUB = 128
D = 512
E = 1024
HEADS = 16
HDIM = 64
NST = 64
NG = 1024
MOST = 128
HALF = MOST // 2
W_IN = 2 * E + 2 * NST
PARTS = 4
QB = 512
BAND = QB + NG


FAR_FIRST = sorted(range(1, N), key=lambda k: -min(k, N - k))


def dot(a, b):
    return jnp.dot(a, b, preferred_element_type=F32)


def dot_nt(a, b):
    return lax.dot_general(a, b, (((1,), (1,)), ((), ())), preferred_element_type=F32)


def dot_tn(a, b):
    return lax.dot_general(a, b, (((0,), (0,)), ((), ())), preferred_element_type=F32)


def iota(shape, dim):
    return lax.broadcasted_iota(jnp.int32, shape, dim)


def two_terms(x):
    high = x.astype(BF16)
    return high, (x - high.astype(F32)).astype(BF16)


def spread(x, table):
    high, low = two_terms(x)
    return dot(high, table) + dot(low, table)


def layer(
    tokens_h,
    gpos_h,
    decay_h,
    w_in_h,
    gain_h,
    w_out_h,
    inner_h,
    w_qkv_h,
    w_back_h,
    out,
    tokens,
    gpos,
    decay,
    w_in,
    gain,
    w_out,
    inner,
    w_qkv,
    total,
    pieces,
    arrived,
    states,
    state_in,
    proj,
    xs,
    inner_y,
    factor,
    hidden,
    place,
    put,
    rows,
    backs,
    qkv,
    packed,
    pick,
    outs,
    firsts,
    sent,
    heads,
    loaded,
    s_tot,
    r_tot,
    s_p,
    r_p,
    s_s,
    r_s,
    s_g,
    r_g,
    s_gs,
    r_gs,
    s_w,
    r_w,
    s_ws,
    r_ws,
    s_h,
    r_h,
):
    me = lax.axis_index("seq")
    chip = me // 2
    core = lax.rem(me, 2)
    sibling = chip * 2 + (1 - core)

    def on_ring(step):
        return lax.rem(chip + step + RING, RING) * 2 + core

    def remote(src, dst, s_sem, r_sem, to):
        return pltpu.make_async_remote_copy(
            src_ref=src,
            dst_ref=dst,
            send_sem=s_sem,
            recv_sem=r_sem,
            device_id={"seq": to},
            device_id_type=MESH,
        )

    def others(body):
        for k in FAR_FIRST:
            body(lax.rem(me + k, N))

    wide = [pl.ds(0, E), pl.ds(2 * E, 2 * NST), pl.ds(E, E)]
    load = {
        name: pltpu.make_async_copy(src, dst, loaded.at[k])
        for k, (name, src, dst) in enumerate(
            (
                ("decay", decay_h, decay),
                ("tokens", tokens_h, tokens),
                *((c, w_in_h.at[:, cols], w_in.at[:, cols]) for c, cols in enumerate(wide)),
                ("back", w_back_h.at[0], backs.at[me]),
                ("gpos", gpos_h, gpos),
                ("gain", gain_h, gain),
                ("out", w_out_h, w_out),
                ("inner", inner_h, inner),
                ("qkv", w_qkv_h.at[0], w_qkv),
            )
        )
    }
    late = (2, "gpos", "gain", "out", "inner", "qkv")
    for name, copy in load.items():
        if name not in late:
            copy.start()
    barrier = pltpu.get_barrier_semaphore()
    others(lambda d: pl.semaphore_signal(barrier, inc=1, device_id={"seq": d}, device_id_type=MESH))

    load["decay"].wait()
    ld = decay[...]
    tri = (iota((TOK, TOK), 0) >= iota((TOK, TOK), 1)).astype(BF16)
    first, rest = two_terms(ld)
    second, third = two_terms(ld - first.astype(F32))
    cum = dot_nt(tri, first) + dot_nt(tri, second) + dot_nt(tri, third)
    end = cum[TOK - 1 : TOK]
    total[me] = jnp.pad(end, ((0, 0), (0, 128 - HEADS)))

    tot_copy = lambda d, src: remote(total.at[src], total.at[src], s_tot.at[d], r_tot.at[src], d)

    def ring_copy(ring, block, part, way, hops, slot):
        buf, parts, s_sem, r_sem, _, _ = ring
        size = buf.shape[1] // parts
        ref = buf.at[block, pl.ds(part * size, size), :]
        return remote(ref, ref, s_sem.at[slot], r_sem.at[parts * block + part], on_ring(hops * way))

    def ring_parts(parts, step):
        for order in range(parts if step < RING // 2 else parts // 2):
            for way in (1, -1):
                yield order, order if way == 1 else (order + parts // 2) % parts, way

    def ring_sends(ring, step):
        parts = ring[1]
        for order, part, way in ring_parts(parts, step):
            block = on_ring(-way * step)
            slot = part * 2 + (way + 1) // 2
            copies = []
            if step == 2 and parts // 4 <= order < parts // 2:
                copies.append(ring_copy(ring, block, part, way, 2, 6 * parts + slot))
            if step < 3 or (step == 3 and order < parts // 4):
                copies.append(ring_copy(ring, block, part, way, 1, 2 * parts * step + slot))
            yield part, way, copies

    def ring_wait(ring, step, part, way):
        ring_copy(ring, on_ring(-way * step), part, way, 1, 0).wait_recv()

    def ring_hand(ring, block):
        buf, _, _, _, s_sib, r_sib = ring
        return remote(buf.at[block], buf.at[block], s_sib.at[block // 2], r_sib.at[block // 2], sibling)

    def ring_ways(step):
        return (1, -1) if 0 < step < RING // 2 else (1,)

    def ring_step(ring, step):
        for part, way, copies in ring_sends(ring, step):
            if step > 0:
                ring_wait(ring, step, part, way)
            for copy in copies:
                copy.start()
        for way in ring_ways(step):
            ring_hand(ring, on_ring(-way * step)).start()

    def ring_sibling_wait(ring, step):
        for way in ring_ways(step):
            ring_hand(ring, (on_ring(-way * step) // 2) * 2 + 1 - core).wait_recv()

    def ring_done(ring):
        for step in range(RING // 2):
            for _, _, copies in ring_sends(ring, step):
                for copy in copies:
                    copy.wait_send()
        for b in range(RING):
            ring_hand(ring, b * 2 + core).wait_send()

    back_ring = (backs, 2, s_w, r_w, s_ws, r_ws)
    row_ring = (rows, PARTS, s_g, r_g, s_gs, r_gs)

    load["tokens"].wait()
    toks = tokens[...]

    def project_in(c):
        load[c].wait()
        proj[:, wide[c]] = dot(toks, w_in[:, wide[c]]).astype(BF16)

    project_in(0)
    project_in(1)
    for name in late:
        load[name].start()

    mids = [cum[SUB // 2 - 1 : SUB // 2], cum[SUB + SUB // 2 - 1 : SUB + SUB // 2]]
    rel = jnp.concatenate([cum[:SUB] - mids[0], cum[SUB:] - mids[1]], axis=0)
    table = (iota((HEADS, E), 1) // HDIM == iota((HEADS, E), 0)).astype(BF16)
    f_in = spread(jnp.exp(rel), table)
    f_out = spread(jnp.exp(-rel), table)
    edge = cum[SUB - 1 : SUB]
    few = jnp.concatenate(
        [mids[0], mids[1], edge - mids[0], end - mids[1], mids[1] - edge, end - edge, end, end], axis=0
    )
    few = spread(jnp.exp(few), table)
    xs[...] = (proj[:, :E].astype(F32) * f_out).astype(BF16)
    bc = proj[:, 2 * E :]
    bmat, cmat = bc[:, :NST], bc[:, NST:]
    low = iota((SUB, SUB), 0) >= iota((SUB, SUB), 1)
    u = [dot_tn(bmat[k * SUB : (k + 1) * SUB], xs[k * SUB : (k + 1) * SUB]) for k in range(2)]
    u0 = u[0] * few[2:3]
    local = (u0 * few[5:6] + u[1] * few[3:4]).astype(BF16)
    for d in range(N):
        r, c = 16 * (d // 4), 256 * (d % 4)
        pieces[d] = local[r : r + 16, c : c + 256]

    p_copy = lambda d, src: remote(pieces.at[d], arrived.at[src], s_p.at[d], r_p.at[src], d)
    pl.semaphore_wait(barrier, N - 1)
    others(lambda d: tot_copy(d, me).start())
    others(lambda d: p_copy(d, me).start())
    load["back"].wait()
    ring_step(back_ring, 0)
    arrived[me] = pieces[me]

    load["gpos"].wait()
    gp = gpos[...]
    base = me * TOK
    before = [jnp.sum((gp < d * TOK).astype(jnp.int32)) for d in range(N)] + [jnp.int32(NG)]
    for d in range(N):
        firsts[d] = before[d]
    here = firsts[me]
    at = base + iota((TOK, 128), 0)
    less = jnp.zeros((TOK, 128), F32)
    same = jnp.zeros((TOK, 128), F32)
    for r in range(8):
        row = gp[r : r + 1]
        less = less + (row < at).astype(F32)
        same = same + (row == at).astype(F32)
    ones = jnp.ones((8, 128), BF16)
    rank = dot_nt(ones, less.astype(BF16))[0:1] - here.astype(F32)
    start = dot_nt(ones, same.astype(BF16))[0:1]
    one_hot = jnp.where((rank == iota((MOST, TOK), 0).astype(F32)) & (start > 0.5), 1.0, 0.0)
    place[...] = one_hot.astype(BF16)
    back_to = one_hot.T.astype(BF16)
    put[...] = jnp.concatenate([back_to, back_to], axis=1)

    u0 = (u0 * few[4:5]).astype(BF16)
    for k in range(2):
        b_k, c_k = bmat[k * SUB : (k + 1) * SUB], cmat[k * SUB : (k + 1) * SUB]
        g = jnp.where(low, dot_nt(c_k, b_k), 0.0).astype(BF16)
        y = dot(g, xs[k * SUB : (k + 1) * SUB])
        if k == 1:
            y = y + dot(c_k, u0)
        inner_y[k * SUB : (k + 1) * SUB] = y
    project_in(2)
    gate = proj[:, E : 2 * E].astype(F32)
    factor[...] = f_in * (gate / (1.0 + jnp.exp(-gate)))

    others(lambda d: tot_copy(d, d).wait_recv())
    lanes = iota((128, 256), 1) // HDIM + 4 * lax.rem(me, 4)
    mine = (lanes == iota((128, 256), 0)).astype(BF16)
    sums = jnp.concatenate([total[d] for d in range(N)], axis=0)
    fades = spread(jnp.exp(sums), mine)

    others(lambda d: p_copy(d, d).wait_recv())
    run = jnp.zeros((16, 256), F32)
    for d in range(N):
        states[d] = run.astype(BF16)
        run = run * fades[d : d + 1] + arrived[d].astype(F32)
    s_copy = lambda d, src: remote(states.at[d], state_in.at[src], s_s.at[d], r_s.at[src], d)
    others(lambda d: s_copy(d, me).start())
    state_in[me] = states[me]

    others(lambda d: s_copy(d, d).wait_recv())
    ring_step(back_ring, 1)

    squares = jnp.zeros((TOK, 1), F32)
    for q in range(4):
        cols = slice(256 * q, 256 * q + 256)
        s = jnp.concatenate([state_in[4 * k + q] for k in range(4)], axis=0).astype(F32)
        s = [(s * few[k : k + 1, cols]).astype(BF16) for k in range(2)]
        carried = jnp.concatenate([dot(cmat[k * SUB : (k + 1) * SUB], s[k]) for k in range(2)], axis=0)
        gated = (inner_y[:, cols] + carried) * factor[:, cols]
        inner_y[:, cols] = gated
        squares = squares + jnp.sum(gated * gated, axis=1, keepdims=True)
    for name in ("gain", "out", "inner", "qkv"):
        load[name].wait()
    scale = lax.rsqrt(squares * (1.0 / E) + 1e-5)
    normed = (inner_y[...] * scale * gain[...]).astype(BF16)
    hid = (toks.astype(F32) + dot(normed, w_out[...])).astype(BF16)
    hidden[...] = hid
    own = dot(place[...], hid)
    own = own * lax.rsqrt(jnp.mean(own * own, axis=1, keepdims=True) + 1e-5) * inner[...]
    rows[me] = own.astype(BF16)

    ring_step(row_ring, 0)

    lane = iota((1, MOST), 1)
    slots = [jnp.where(lane + before[d] < before[d + 1], lane + before[d], -1) for d in range(N)]
    for p in range(NG // QB):
        for t in range(BAND // MOST):
            d = p * QB // MOST + t
            want = iota((QB, MOST), 0) + p * QB
            pick[p, :, t * MOST : (t + 1) * MOST] = (want == slots[d]).astype(BF16)
    outs[...] = jnp.zeros_like(outs)

    def project(block):
        qkv[pl.ds(pl.multiple_of(block * MOST, MOST), MOST), :] = dot_nt(rows[block], w_qkv[...]).astype(BF16)

    project(me)
    for step in range(1, RING // 2 + 1):
        ring_step(row_ring, step)
        if step == 4:
            ring_step(back_ring, 2)
        ring_sibling_wait(row_ring, step - 1)
        for way in ring_ways(step - 1):
            project((on_ring(-way * (step - 1)) // 2) * 2 + 1 - core)
        for way in ring_ways(step):
            project(on_ring(-way * step))
    ring_sibling_wait(row_ring, RING // 2)
    project((on_ring(RING // 2) // 2) * 2 + 1 - core)

    for p in range(NG // QB):
        packed[p * QB : (p + 1) * QB] = dot(pick[p], qkv[p * QB : p * QB + BAND]).astype(BF16)

    h_copy = lambda d, src: remote(sent.at[d], heads.at[src], s_h.at[d], r_h.at[src], d)

    def pack_head(d):
        block = outs[pl.ds(firsts[d], MOST), :]
        return jnp.concatenate([block[:HALF], block[HALF:]], axis=1).astype(BF16)

    def ship(d):
        sent[d] = pack_head(d)
        h_copy(d, me).start()

    corner = iota((QB, QB), 0) >= iota((QB, QB), 1)
    shipped = 0
    for p in range(NG // QB):
        upto = (p + 1) * QB
        query = packed[p * QB : upto, :HDIM] * jnp.asarray(HDIM**-0.5, BF16)
        scores = dot_nt(query, packed[:upto, HDIM : 2 * HDIM])
        edge = jnp.where(corner, scores[:, p * QB :], -jnp.inf)
        scores = edge if p == 0 else jnp.concatenate([scores[:, : p * QB], edge], axis=1)
        expo = jnp.exp(scores - jnp.max(scores, axis=1, keepdims=True))
        weight = 1.0 / jnp.sum(expo, axis=1, keepdims=True)
        outs[p * QB : upto] = dot(expo.astype(BF16), packed[:upto, 2 * HDIM :]) * weight
        if upto < NG:
            for d in range(shipped, upto // MOST):
                pl.when(me != d)(functools.partial(ship, d))
            shipped = upto // MOST
    for k in FAR_FIRST:
        d = lax.rem(me + k, N)
        pl.when(d >= shipped)(functools.partial(ship, d))
    heads[me] = pack_head(me)

    for step in (3, 4):
        ring_step(back_ring, step)
    for step in range(RING // 2 + 1):
        ring_sibling_wait(back_ring, step)

    others(lambda d: h_copy(d, d).wait_recv())
    left = iota((HALF, 128), 1) < HDIM
    tops, bottoms = [], []
    for h in range(0, N, 2):
        a, b = heads[h].astype(F32), heads[h + 1].astype(F32)
        tops.append(jnp.where(left, a, pltpu.roll(b, HDIM, 1)).astype(BF16))
        bottoms.append(jnp.where(left, pltpu.roll(a, HDIM, 1), b).astype(BF16))
    joined = jnp.concatenate([jnp.concatenate(tops, axis=1), jnp.concatenate(bottoms, axis=1)], axis=0)
    back = dot(joined, backs[...].reshape(N * HDIM, D))
    placed = dot(put[...], jnp.concatenate(two_terms(back), axis=0))
    out[...] = (hidden[...].astype(F32) + placed).astype(BF16)

    others(lambda d: tot_copy(d, me).wait_send())
    others(lambda d: p_copy(d, me).wait_send())
    others(lambda d: s_copy(d, me).wait_send())
    others(lambda d: h_copy(d, me).wait_send())
    ring_done(back_ring)
    ring_done(row_ring)


def shards(tokens, group_pos, log_decay, in_weight, norm_gain, out_weight, inner_gain, qkv_weight, attn_out):
    vmem = pl.BlockSpec(memory_space=pltpu.VMEM)
    hbm = pl.BlockSpec(memory_space=pltpu.HBM)
    dma = pltpu.SemaphoreType.DMA
    return pl.pallas_call(
        layer,
        out_shape=jax.ShapeDtypeStruct((TOK, D), BF16),
        in_specs=[hbm] * 9,
        out_specs=vmem,
        scratch_shapes=[
            pltpu.VMEM((TOK, D), BF16),
            pltpu.VMEM((8, NG // 8), jnp.int32),
            pltpu.VMEM((HEADS, TOK), F32),
            pltpu.VMEM((D, W_IN), BF16),
            pltpu.VMEM((1, E), F32),
            pltpu.VMEM((E, D), BF16),
            pltpu.VMEM((1, D), F32),
            pltpu.VMEM((3 * HDIM, D), BF16),
            pltpu.VMEM((N, 1, 128), F32),
            pltpu.VMEM((N, 16, 256), BF16),
            pltpu.VMEM((N, 16, 256), BF16),
            pltpu.VMEM((N, 16, 256), BF16),
            pltpu.VMEM((N, 16, 256), BF16),
            pltpu.VMEM((TOK, W_IN), BF16),
            pltpu.VMEM((TOK, E), BF16),
            pltpu.VMEM((TOK, E), F32),
            pltpu.VMEM((TOK, E), F32),
            pltpu.VMEM((TOK, D), BF16),
            pltpu.VMEM((MOST, TOK), BF16),
            pltpu.VMEM((TOK, 2 * MOST), BF16),
            pltpu.VMEM((N, MOST, D), BF16),
            pltpu.VMEM((N, HDIM, D), BF16),
            pltpu.VMEM((N * MOST, 3 * HDIM), BF16),
            pltpu.VMEM((NG, 3 * HDIM), BF16),
            pltpu.VMEM((NG // QB, QB, BAND), BF16),
            pltpu.VMEM((NG + MOST, HDIM), F32),
            pltpu.SMEM((N,), jnp.int32),
            pltpu.VMEM((N, HALF, 128), BF16),
            pltpu.VMEM((N, HALF, 128), BF16),
        ]
        + [dma((11,))]
        + [dma((N,))] * 6
        + [dma((RING * PARTS,)), dma((N * PARTS,)), dma((RING,)), dma((RING,))] * 2
        + [dma((N,))] * 2,
        compiler_params=pltpu.CompilerParams(
            collective_id=0, has_side_effects=True, vmem_limit_bytes=48 * 2**20
        ),
    )(
        *(
            pltpu.with_memory_space_constraint(x, pltpu.HBM)
            for x in (
                tokens,
                group_pos.reshape(8, NG // 8),
                log_decay.T,
                in_weight,
                norm_gain.reshape(1, E),
                out_weight,
                inner_gain.reshape(1, D),
                qkv_weight.transpose(0, 2, 1),
                attn_out,
            )
        )
    )


def solution(mesh):
    return jax.shard_map(
        shards,
        mesh=mesh,
        in_specs=(
            P(("grp", "seq"), None),
            P("grp"),
            P(("grp", "seq"), None),
            P(),
            P(),
            P(),
            P(),
            P("seq", None, None),
            P("seq", None, None),
        ),
        out_specs=P(("grp", "seq"), None),
        check_vma=False,
    )
```
